256 devices in a mesh: row: 4 (over z_lo), col: 8 (over y, z_hi), head: 8 (over x, core).
Axes of the slice: x: 4, y: 4, z: 8 (z_hi: 2, z_lo: 4; z = z_hi * 4 + z_lo), core: 2. Of those that a mesh axis runs over, the one named last changes fastest.
Arguments:
- hidden_in: bfloat16 [4, 8, 384, 3072], P('row', 'col', None, 'head'), may hold values from -6 to 6
- mod_shift: float32 [3072], replicated, may hold values from -3 to 3
- mod_scale: float32 [3072], replicated, may hold values from -0.5 to 1
- mod_gate: float32 [3072], P('head'), may hold values from 0.5 to 2
- w_qkv: bfloat16 [3072, 3, 3072], P(None, None, 'head'), may hold values from -1 to 1
- query_gain: float32 [128], replicated, may hold values from 0.5 to 8
- key_gain: float32 [128], replicated, may hold values from 0.5 to 8
- w_out: bfloat16 [3072, 3072], P('head'), may hold values from -0.15625 to 0.15625
- window: int32 [4, 8, 9], P('row', 'col'), may hold values from 0 to 1, as said below
Outputs:
- hidden_out: bfloat16 [4, 8, 384, 3072], P('row', 'col', None, 'head')
The draws below stay inside these ranges and needn't reach their ends.
Inputs may be any that keep to these rules, and one draw needn't show every extreme that they name: `window`: 0 for neighbours outside the tile grid; the centre entry is 1; other entries are 0 or 1.
All inputs are finite; a program needn't handle non-finite values.
Results may differ from the reference program's by a relative error of at most 0.018.
The reference program's roundings to bfloat16 on the way count: a program that leaves them out, or rounds other values in their place, can miss the bound.
Values may be sent and summed in bfloat16 or wider, within the bound.
A program may use at most 128 MiB of HBM per device.

```python
import math
import jax
import jax.numpy as jnp
from jax import lax

D = 3072
HEADS = 24
HD = 128
TILE = 384
NR = 4
NC = 8
N_HEAD = 8


def draw_window(key, part):
    key = jax.random.fold_in(key, 7)
    rows = jnp.arange(NR, dtype=jnp.int32)[:, None, None]
    cols = jnp.arange(NC, dtype=jnp.int32)[None, :, None]
    offset = jnp.arange(9, dtype=jnp.int32)[None, None, :]
    drow = offset // 3 - 1
    dcol = offset % 3 - 1
    inside = (rows + drow >= 0) & (rows + drow < NR) & (cols + dcol >= 0) & (cols + dcol < NC)
    keep = jax.random.randint(key, (NR, NC, 9), 0, 5) > 0
    keep = keep | (offset == 4)
    return (inside & keep).astype(jnp.int32)


def log_range(key, lower, upper):
    level = jax.random.uniform(key, (HD,), jnp.float32)
    return jnp.exp(jnp.log(lower) + level * (jnp.log(upper) - jnp.log(lower)))


def draw_query_gain(key, part):
    key = jax.random.fold_in(key, 17)
    return log_range(key, 0.5, 8.0)


def draw_key_gain(key, part):
    key = jax.random.fold_in(key, 19)
    return log_range(key, 0.5, 8.0)


def draw_hidden_in(key, part):
    key = jax.random.fold_in(key, 11)
    noise_key = jax.random.fold_in(key, 0)
    noise = jax.random.normal(noise_key, (NR, NC, TILE, D), jnp.float32)
    return jnp.clip(noise, -6.0, 6.0).astype(jnp.bfloat16)


def draw_w_qkv(key, part):
    key = jax.random.fold_in(key, 13)
    base_key = jax.random.fold_in(key, 0)
    base = jnp.clip(jax.random.normal(base_key, (D, 3, HEADS * HD), jnp.float32), -6.0, 6.0) / jnp.sqrt(jnp.float32(D))
    return base.astype(jnp.bfloat16)


def strengthened(drawn, own_key, source, target, blocks, factor):
    def block_of(position):
        return (jnp.arange(drawn.shape[position]) // (drawn.shape[position] // blocks)).reshape((-1,) + (1,) * (drawn.ndim - 1 - position))

    one_side = jax.random.permutation(own_key, blocks)[block_of(target)]
    far = (block_of(target) + blocks // 2) % blocks
    return jnp.where((block_of(source) == one_side) | (block_of(source) == far), factor * drawn, drawn)


def shard_levels(stream_key, dims, cuts, low, high):
    loudness = 1.0
    for position, parts in cuts:
        draws = jax.random.uniform(jax.random.fold_in(jax.random.fold_in(stream_key, 6), position), (parts,), jnp.float32, low / len(cuts), high / len(cuts))
        loudness = loudness * jnp.repeat(jnp.exp(draws), dims[position] // parts).reshape((-1,) + (1,) * (len(dims) - 1 - position))
    return loudness


def centred(own_key, dims, scale, limit, shards=(), held_as=jnp.bfloat16):
    values = scale * jax.random.normal(own_key, dims, jnp.float32)
    if shards:
        values = values * shard_levels(own_key, dims, shards, -0.22, 0.18)
    return jnp.clip(values, -limit, limit).astype(held_as)


def heavy_noise(key, extent, scale, limit, cuts, heavy, kind=jnp.bfloat16):
    drawn = scale * jax.random.normal(key, extent, jnp.float32)
    if cuts:
        drawn = drawn * shard_levels(key, extent, cuts, -0.22, 0.18)
    return jnp.clip(strengthened(drawn, jax.random.fold_in(key, 3), *heavy), -limit, limit).astype(kind)


def setup_inputs(seed: int = 0) -> dict:
    key_list = jax.random.split(jax.random.key(seed), 10)
    hidden_in = draw_hidden_in(jax.random.fold_in(key_list[9], 71), 0)
    mod_shift = centred(key_list[1], (D,), 0.5, 3.0, (), jnp.float32)
    mod_scale = jnp.clip(jax.random.uniform(key_list[2], (D,), jnp.float32, -0.5, 1.0), -0.5, 1.0)
    mod_gate = jnp.clip(jnp.exp(math.log(2.0) - 1.3862944 * jax.random.uniform(key_list[3], (D,), jnp.float32) ** shard_levels(key_list[3], (D,), ((0, 8),), -0.2, 0.2)), 0.5, 2.0)
    w_qkv = draw_w_qkv(jax.random.fold_in(key_list[9], 71), 0)
    query_gain = draw_query_gain(jax.random.fold_in(key_list[9], 71), 0)
    key_gain = draw_key_gain(jax.random.fold_in(key_list[9], 71), 0)
    w_out = heavy_noise(key_list[7], (HEADS * HD, D), (HEADS * HD) ** -0.5, 0.15625, ((0, 8),), (0, 1, 8, 2.0))
    window = draw_window(jax.random.fold_in(key_list[9], 71), 0)
    return dict(hidden_in=hidden_in, mod_shift=mod_shift, mod_scale=mod_scale, mod_gate=mod_gate, w_qkv=w_qkv, query_gain=query_gain, key_gain=key_gain, w_out=w_out, window=window)


def head_norm(values, gain):
    return values * lax.rsqrt(lax.optimization_barrier(jnp.mean(values * values, axis=-1, keepdims=True)) + 1e-06) * gain

def reference(hidden_in, mod_shift, mod_scale, mod_gate, w_qkv, query_gain, key_gain, w_out, window):
    xfloat = hidden_in.astype(jnp.float32)
    center = lax.optimization_barrier(jnp.mean(xfloat, axis=-1, keepdims=True))
    spread = lax.optimization_barrier(jnp.mean((xfloat - center) ** 2, axis=-1, keepdims=True))
    normed = ((xfloat - center) * lax.rsqrt(spread + 1e-06) * (1.0 + mod_scale) + mod_shift).astype(jnp.bfloat16)
    tokens = NR * NC * TILE
    qkv = jnp.dot(normed.reshape(tokens, D), w_qkv.reshape(D, 3 * HEADS * HD), preferred_element_type=jnp.float32)
    qkv = qkv.reshape(NR, NC, TILE, 3, HEADS, HD)
    query = head_norm(qkv[:, :, :, 0], query_gain).astype(jnp.bfloat16)
    keyed = head_norm(qkv[:, :, :, 1], key_gain).astype(jnp.bfloat16)
    valued = qkv[:, :, :, 2].astype(jnp.bfloat16)
    padded = jnp.pad(jnp.stack([keyed, valued], axis=3), ((1, 1), (1, 1), (0, 0), (0, 0), (0, 0), (0, 0)))
    inverse = 1.0 / jnp.sqrt(jnp.float32(HD))

    def one_tile(index):
        trow = (index // NC).astype(jnp.int32)
        tcol = (index % NC).astype(jnp.int32)
        blocks = []
        for offset in range(9):
            drow = offset // 3
            dcol = offset % 3
            piece = lax.dynamic_slice(padded, (trow + drow, tcol + dcol, jnp.int32(0), jnp.int32(0), jnp.int32(0), jnp.int32(0)), (1, 1, TILE, 2, HEADS, HD))
            blocks.append(piece[0, 0])
        stacked = jnp.stack(blocks, axis=0)
        qtile = lax.dynamic_slice(query, (trow, tcol, jnp.int32(0), jnp.int32(0), jnp.int32(0)), (1, 1, TILE, HEADS, HD))[0, 0]
        valid = lax.dynamic_slice(window, (trow, tcol, jnp.int32(0)), (1, 1, 9))[0, 0]
        scores = jnp.einsum('qhd,jkhd->hqjk', qtile.astype(jnp.float32), stacked[:, :, 0].astype(jnp.float32)) * inverse
        scores = jnp.where(valid[None, None, :, None] > 0, scores, -1e+30)
        top = lax.optimization_barrier(jnp.max(scores, axis=(2, 3), keepdims=True))
        weights = jnp.exp(scores - top)
        total = lax.optimization_barrier(jnp.sum(weights, axis=(2, 3), keepdims=True))
        probs = (weights / total).astype(jnp.bfloat16)
        result = jnp.einsum('hqjk,jkhd->qhd', probs.astype(jnp.float32), stacked[:, :, 1].astype(jnp.float32))
        return result.astype(jnp.bfloat16)
    attn = lax.map(one_tile, jnp.arange(NR * NC, dtype=jnp.int32))
    attn = attn.reshape(tokens, HEADS * HD)
    group = HEADS // N_HEAD * HD
    proj = jnp.zeros((tokens, D), jnp.float32)
    for index in range(N_HEAD):
        partial_term = jnp.dot(attn[:, index * group:(index + 1) * group], w_out[index * group:(index + 1) * group], preferred_element_type=jnp.float32)
        rounded = lax.optimization_barrier(partial_term.astype(jnp.bfloat16))
        proj = proj + rounded.astype(jnp.float32)
    result = xfloat + mod_gate * proj.reshape(NR, NC, TILE, D)
    return result.astype(jnp.bfloat16)
```

```python
import functools
import math

import jax
import jax.numpy as jnp
from jax import lax
from jax.experimental import pallas as pl
from jax.experimental.pallas import tpu as pltpu
from jax.sharding import PartitionSpec as P

MESH = pl.DeviceIdType.MESH
F32 = jnp.float32
BF16 = jnp.bfloat16
HD = 128
NH = 3
NG = 8
T = 384
W = NH * HD
D = NG * W
ROWS = 4
OWN, BELOW, ABOVE, FAR = 4, 5, 6, 7
SLOTS = 10
SCALE = math.log2(math.e) / math.sqrt(HD)
NEG = -1e30
LAG = 3


def kernel(
    x_ref, shift_ref, scale_ref, gate_ref, w_hbm, qg_ref, kg_ref, wo_hbm, win_ref, out_ref,
    hg, nb, wq, kv, qs, acc, m_s, l_s, wo, at,
    w_sem, own_sem, ag_s, agf_s, ag_r, kv_s, y_s, kv_r, wo_s, wo_r, at_s, atf_s, at_r,
):
    r = lax.axis_index("row")
    c = lax.axis_index("col")
    g = lax.axis_index("head")
    y, zh = c // 2, c % 2
    core = g % 2
    mate = g + 1 - 2 * core
    peers = [lax.rem(g + 2, NG), lax.rem(g + 6, NG), lax.rem(g + 4, NG)]
    z_next = (jnp.where(r < 3, r + 1, 0), jnp.where(r < 3, c, c + 1 - 2 * zh), g)
    z_prev = (jnp.where(r > 0, r - 1, 3), jnp.where(r > 0, c, c + 1 - 2 * zh), g)
    y_next = (r, lax.rem(c + 2, 8), g)
    y_prev = (r, lax.rem(c + 6, 8), g)
    y_out = (r, lax.rem(jnp.where(zh == 0, c + 2, c + 6), 8), g)
    has_out = jnp.where(zh == 0, y < 3, y > 0)
    has_in = jnp.where(zh == 0, y > 0, y < 3)

    def on_head(i):
        return (r, c, i)

    w_copies = [pltpu.make_async_copy(w_hbm.at[j], wq.at[j], w_sem.at[j]) for j in range(3)]
    for j in (1, 2, 0):
        w_copies[j].start()

    def columns(i):
        return wo_hbm.at[:, pl.ds(pl.multiple_of(i * W, W), W)]

    wo_own = pltpu.make_async_copy(columns(g), wo.at[g], own_sem)
    wo_own.start()

    barrier = pltpu.get_barrier_semaphore()
    for i in range(1, NG):
        pl.semaphore_signal(barrier, inc=1, device_id=on_head(lax.rem(g + i, NG)), device_id_type=MESH)
    for dev in (z_next, z_prev, y_next, y_prev):
        pl.semaphore_signal(barrier, inc=1, device_id=dev, device_id_type=MESH)
    pl.semaphore_wait(barrier, NG - 1 + 4)

    def ag_copy(src, slot, send, dev):
        return pltpu.make_async_remote_copy(
            src_ref=src, dst_ref=hg.at[slot], send_sem=send, recv_sem=ag_r.at[slot],
            device_id=on_head(dev), device_id_type=MESH)

    firsts = [ag_copy(x_ref, g, ag_s.at[i], dev) for i, dev in enumerate(peers + [mate])]
    for copy in firsts:
        copy.start()
    hg[g] = x_ref[...]
    forwards = []
    for i, dev in enumerate(peers):
        ag_copy(x_ref, dev, ag_s.at[i], dev).wait_recv()
        forward = ag_copy(hg.at[dev], dev, agf_s.at[i], mate)
        forward.start()
        forwards.append(forward)
    ag_copy(x_ref, mate, ag_s.at[3], mate).wait_recv()
    for i, dev in enumerate(peers):
        other = dev + 1 - 2 * core
        ag_copy(x_ref, other, agf_s.at[i], mate).wait_recv()

    step = 32

    def norm_rows(i, _):
        rows = pl.ds(pl.multiple_of(i * step, step), step)
        parts = [hg[j, rows, :].astype(F32) for j in range(NG)]
        total = parts[0]
        for part in parts[1:]:
            total = total + part
        center = jnp.sum(total, axis=-1, keepdims=True) * (1.0 / D)
        squares = None
        for part in parts:
            off = part - center
            squares = off * off if squares is None else squares + off * off
        spread = jnp.sum(squares, axis=-1, keepdims=True) * (1.0 / D)
        inv = lax.rsqrt(spread + 1e-6)
        for j in range(NG):
            cols = slice(j * W, (j + 1) * W)
            nb[rows, cols] = (
                (parts[j] - center) * inv * (1.0 + scale_ref[:, cols]) + shift_ref[:, cols]
            ).astype(BF16)
        return 0

    lax.fori_loop(0, T // step, norm_rows, 0)

    def kv_copy(src, dst, h, part, send, dev):
        return pltpu.make_async_remote_copy(
            src_ref=kv.at[src, h, part], dst_ref=kv.at[dst, h, part],
            send_sem=send, recv_sem=kv_r.at[dst, h, part],
            device_id=dev, device_id_type=MESH)

    def send_own(h, part):
        kv_copy(OWN, jnp.where(r == 0, 0, BELOW), h, part, kv_s.at[0, 0, h, part], z_prev).start()
        kv_copy(OWN, jnp.where(r == 3, 3, ABOVE), h, part, kv_s.at[1, 0, h, part], z_next).start()

    def project(j):
        w_copies[j].wait()
        return jnp.dot(nb[...], wq[j], preferred_element_type=F32)

    def head_norm(values, gain):
        mean = jnp.mean(values * values, axis=-1, keepdims=True)
        return (values * lax.rsqrt(mean + 1e-6) * gain).astype(BF16)

    keys = project(1)
    for h in range(NH):
        kv[OWN, h, 0] = head_norm(keys[:, h * HD:(h + 1) * HD], kg_ref[...])
        send_own(h, 0)
    values = project(2)
    for h in range(NH):
        kv[OWN, h, 1] = values[:, h * HD:(h + 1) * HD].astype(BF16)
        send_own(h, 1)
    queries = project(0)
    for h in range(NH):
        qs[h] = head_norm(queries[:, h * HD:(h + 1) * HD], qg_ref[...])

    def wo_copy(i):
        dev = lax.rem(g + i, NG)
        return pltpu.make_async_remote_copy(
            src_ref=columns(dev), dst_ref=wo.at[g], send_sem=wo_s.at[i], recv_sem=wo_r.at[g],
            device_id=on_head(dev), device_id_type=MESH)

    for i in range(1, NG):
        wo_copy(i).start()

    m_s[...] = jnp.full_like(m_s, NEG)
    l_s[...] = jnp.zeros_like(l_s)
    acc[...] = jnp.zeros_like(acc)
    block = 128

    def attend(slot, h, offset):
        kept = win_ref[offset] > 0
        k = kv[slot, h, 0]
        v = kv[slot, h, 1]
        for i in range(T // block):
            rows = slice(i * block, (i + 1) * block)
            s = lax.dot_general(
                qs[h, rows, :], k, (((1,), (1,)), ((), ())), preferred_element_type=F32)
            top = jnp.max(s, axis=-1, keepdims=True) * SCALE
            old = m_s[h, rows, :]
            new = jnp.maximum(old, jnp.where(kept, top, NEG))
            decay = jnp.exp2(old - new)
            less = jnp.where(kept, new, -NEG)
            p = jnp.exp2(s * SCALE - jnp.concatenate([less] * (T // HD), axis=1))
            m_s[h, rows, :] = new
            l_s[h, rows, :] = l_s[h, rows, :] * decay + jnp.sum(p, axis=-1, keepdims=True)
            acc[h, rows, :] = acc[h, rows, :] * decay + jnp.dot(
                p.astype(BF16), v, preferred_element_type=F32)

    def own_tile(h, _):
        attend(OWN, h, 4)
        return 0

    lax.fori_loop(0, NH, own_tile, 0)

    def arrived(slot, h, part):
        kv_copy(OWN, slot, h, part, kv_s.at[0, 0, h, part], z_prev).wait_recv()

    near = jnp.where(r >= 2, 0, 1)
    lag = jnp.where((r == 0) | (r == 3), LAG, 1)

    def x_slot(stream, e):
        return jnp.where(stream == 0, e // NH, 3 - e // NH)

    def inside(slot):
        return (slot >= r - 1) & (slot <= r + 1)

    def x_event(stream, e):
        slot, h, k = x_slot(stream, e), lax.rem(e, NH), e // NH
        for part in range(2):
            arrived(slot, h, part)

            @pl.when((stream == 0) & (r > 0))
            def _():
                kv_copy(slot, slot, h, part, kv_s.at[0, 1 + k, h, part], z_prev).start()

            @pl.when((stream == 1) & (r < 3))
            def _():
                kv_copy(slot, slot, h, part, kv_s.at[1, 1 + k, h, part], z_next).start()

            @pl.when(inside(slot) & has_out)
            def _():
                turn = slot - r + 1
                kv_copy(slot, FAR + turn, h, part, y_s.at[turn, h, part], y_out).start()

    def valid_event(e):
        return (e >= 0) & (e < 2 * NH)

    def at_copy(slot, h, send, dev):
        return pltpu.make_async_remote_copy(
            src_ref=at.at[slot, h], dst_ref=at.at[slot, h], send_sem=send, recv_sem=at_r.at[slot, h],
            device_id=on_head(dev), device_id_type=MESH)

    def finish_head(h):
        at[g, h] = (acc[h] / l_s[h]).astype(BF16)
        for i, dev in enumerate(peers + [mate]):
            at_copy(g, h, at_s.at[i, h], dev).start()

    def pass_head(h):
        for i, dev in enumerate(peers):
            at_copy(dev, h, at_s.at[i, h], dev).wait_recv()
            at_copy(dev, h, atf_s.at[i, h], mate).start()

    def tick(t, _):
        @pl.when(t < NH)
        def _():
            @pl.when(r < 3)
            def _():
                for part in range(2):
                    arrived(BELOW, t, part)

                    @pl.when(r == 0)
                    def _():
                        kv_copy(BELOW, 1, t, part, kv_s.at[0, 1, t, part], z_prev).start()

            @pl.when(r > 0)
            def _():
                for part in range(2):
                    arrived(ABOVE, t, part)

                    @pl.when(r == 3)
                    def _():
                        kv_copy(ABOVE, 2, t, part, kv_s.at[1, 1, t, part], z_next).start()

        e_near, e_far = t, t - lag

        @pl.when(valid_event(e_near))
        def _():
            x_event(near, e_near)

        @pl.when(valid_event(e_far))
        def _():
            x_event(1 - near, e_far)

        def compute(i, _):
            stream = jnp.where(lax.rem(i, 2) == 0, near, 1 - near)
            e = jnp.where(lax.rem(i, 2) == 0, t, t - lag) - jnp.where(i >= 4, 1, 0)
            e_ok = valid_event(e)
            e = jnp.where(e_ok, e, 0)
            slot_x = x_slot(stream, e)
            turn = slot_x - r + 1
            is_far = i >= 4
            slot = jnp.where(
                i < 2, jnp.where(i == 0, BELOW, ABOVE), jnp.where(is_far, FAR + turn, slot_x))
            h = jnp.where(i < 2, t, lax.rem(e, NH))
            ok = jnp.where(
                i < 2,
                (t < NH) & jnp.where(i == 0, r < 3, r > 0),
                e_ok & inside(slot_x) & (jnp.logical_not(is_far) | has_in))
            side = jnp.where(is_far, 2 * zh, 2 - 2 * zh)
            offset = jnp.where(i < 2, jnp.where(i == 0, 7, 1), 3 * turn + side)

            @pl.when(ok)
            def _():
                @pl.when(is_far)
                def _():
                    arrived(slot, h, 0)
                    arrived(slot, h, 1)

                attend(slot, h, offset)

            return 0

        lax.fori_loop(0, 6, compute, 0)
        done = t - lag - NH - 1

        @pl.when((done >= 0) & (done < NH))
        def _():
            finish_head(done)

            @pl.when(done > 0)
            def _():
                pass_head(done - 1)

        return 0

    lax.fori_loop(0, 2 * NH + LAG + 1, tick, 0)
    pass_head(NH - 1)
    for h in range(NH):
        at_copy(mate, h, at_s.at[3, h], mate).wait_recv()
        for i, dev in enumerate(peers):
            at_copy(dev + 1 - 2 * core, h, atf_s.at[i, h], mate).wait_recv()
    wo_own.wait()
    for i in range(1, NG):
        src = lax.rem(g + i, NG)
        pltpu.make_async_remote_copy(
            src_ref=columns(src), dst_ref=wo.at[src], send_sem=wo_s.at[i], recv_sem=wo_r.at[src],
            device_id=on_head(src), device_id_type=MESH).wait_recv()


    def group(i, total):
        a = jnp.concatenate([at[i, h] for h in range(NH)], axis=1)
        part = jnp.dot(a, wo[i], preferred_element_type=F32)
        return total + part.astype(BF16).astype(F32)

    proj = lax.fori_loop(0, NG, group, jnp.zeros((T, W), F32))
    out_ref[...] = (x_ref[...].astype(F32) + gate_ref[...] * proj).astype(BF16)

    for copy in firsts + forwards:
        copy.wait_send()
    for i in range(1, NG):
        wo_copy(i).wait_send()
    for h in range(NH):
        for i, dev in enumerate(peers + [mate]):
            at_copy(g, h, at_s.at[i, h], dev).wait_send()
        for i, dev in enumerate(peers):
            at_copy(dev, h, atf_s.at[i, h], mate).wait_send()

    def sent(i, _):
        h, part = i // 2, lax.rem(i, 2)
        for k in range(3):
            @pl.when((r > 0) | (k < 2))
            def _():
                kv_copy(OWN, OWN, h, part, kv_s.at[0, k, h, part], z_prev).wait_send()

            @pl.when((r < 3) | (k < 2))
            def _():
                kv_copy(OWN, OWN, h, part, kv_s.at[1, k, h, part], z_next).wait_send()

            j = r - 1 + k

            @pl.when(has_out & (j >= 0) & (j < ROWS))
            def _():
                kv_copy(OWN, OWN, h, part, y_s.at[k, h, part], y_out).wait_send()

        return 0

    lax.fori_loop(0, 2 * NH, sent, 0)


def on_device(
    hidden_in, mod_shift, mod_scale, mod_gate, w_qkv, query_gain, key_gain, w_out, window
):
    vmem = pl.BlockSpec(memory_space=pltpu.VMEM)
    hbm = pl.BlockSpec(memory_space=pl.ANY)
    smem = pl.BlockSpec(memory_space=pltpu.SMEM)
    dma = pltpu.SemaphoreType.DMA
    out = pl.pallas_call(
        kernel,
        out_shape=jax.ShapeDtypeStruct((T, W), BF16),
        in_specs=[vmem, vmem, vmem, vmem, hbm, vmem, vmem, hbm, smem],
        out_specs=vmem,
        scratch_shapes=[
            pltpu.VMEM((NG, T, W), BF16),
            pltpu.VMEM((T, D), BF16),
            pltpu.VMEM((3, D, W), BF16),
            pltpu.VMEM((SLOTS, NH, 2, T, HD), BF16),
            pltpu.VMEM((NH, T, HD), BF16),
            pltpu.VMEM((NH, T, HD), F32),
            pltpu.VMEM((NH, T, HD), F32),
            pltpu.VMEM((NH, T, HD), F32),
            pltpu.VMEM((NG, W, W), BF16),
            pltpu.VMEM((NG, NH, T, HD), BF16),
            dma((3,)), dma, dma((4,)), dma((3,)), dma((NG,)),
            dma((2, 3, NH, 2)), dma((3, NH, 2)), dma((SLOTS, NH, 2)),
            dma((NG,)), dma((NG,)), dma((4, NH)), dma((3, NH)), dma((NG, NH)),
        ],
        compiler_params=pltpu.CompilerParams(
            collective_id=0, has_side_effects=True, vmem_limit_bytes=48 * 1024 * 1024),
        cost_estimate=pl.CostEstimate(
            flops=6_000_000_000, bytes_accessed=10_000_000, transcendentals=4_000_000),
        name="tile_attention",
    )(
        hidden_in.reshape(T, W),
        mod_shift.reshape(1, D),
        mod_scale.reshape(1, D),
        mod_gate.reshape(1, W),
        jnp.transpose(w_qkv, (1, 0, 2)),
        query_gain.reshape(1, HD),
        key_gain.reshape(1, HD),
        w_out,
        window.reshape(9),
    )
    return out.reshape(hidden_in.shape)


def solution(mesh):
    in_specs = (
        P("row", "col", None, "head"),
        P(),
        P(),
        P("head"),
        P(None, None, "head"),
        P(),
        P(),
        P("head", None),
        P("row", "col", None),
    )
    out_specs = P("row", "col", None, "head")
    return jax.shard_map(
        on_device, mesh=mesh, in_specs=in_specs, out_specs=out_specs, check_vma=False
    )
```

```python
import functools
import math

import jax
import jax.numpy as jnp
from jax import lax
from jax.experimental import pallas as pl
from jax.experimental.pallas import tpu as pltpu
from jax.sharding import PartitionSpec as P

MESH = pl.DeviceIdType.MESH
F32 = jnp.float32
BF16 = jnp.bfloat16
HD = 128
NH = 3
NG = 8
T = 384
W = NH * HD
D = NG * W
ROWS = 4
OWN, MATE = 6, 7
SLOTS = 10
SCALE = math.log2(math.e) / math.sqrt(HD)
NEG = -1e30
EVENTS = 9
LAG_OWN, LAG = 1, 2
LAG_BACK = 1


def kernel(
    x_hbm, shift_hbm, scale_hbm, w_hbm, qg_hbm, kg_hbm, wo_hbm, win_hbm, out_ref,
    shift_ref, scale_ref, qg_ref, kg_ref, win_ref, small_sem, hg, nb, wq, kv, qs, acc, m_s, l_s, wo, at, mk, back, stats,
    w_sem, own_sem, ag_s, agx_s, agf_s, ag_r, kv_s, z_s, mate_s, kv_r, q_s, q_r, mk_s, mk_r, back_s, back_r, wo_s, wo_r, at_s, atf_s, at_r,
):
    r = lax.axis_index("row")
    c = lax.axis_index("col")
    g = lax.axis_index("head")
    y, zh = c // 2, c % 2
    core = g % 2
    mate = g + 1 - 2 * core
    right, left = lax.rem(g + 2, NG), lax.rem(g + 6, NG)
    peers = [lax.rem(g + 2, NG), lax.rem(g + 6, NG), lax.rem(g + 4, NG)]
    x0 = g - core
    z_next = (jnp.where(r < 3, r + 1, 0), jnp.where(r < 3, c, c + 1 - 2 * zh))
    z_prev = (jnp.where(r > 0, r - 1, 3), jnp.where(r > 0, c, c + 1 - 2 * zh))
    rank = jnp.where(core == 0, r, 3 - r)
    onward = (
        jnp.where(core == 0, z_prev[0], z_next[0]), jnp.where(core == 0, z_prev[1], z_next[1]), g)
    y_to = lax.rem(jnp.where(zh == 0, c + 2, c + 6), 8)
    y_from = lax.rem(jnp.where(zh == 0, c + 6, c + 2), 8)
    has_out = jnp.where(zh == 0, y < 3, y > 0)
    has_in = jnp.where(zh == 0, y > 0, y < 3)

    def on_head(i):
        return (r, c, i)

    smalls = [
        pltpu.make_async_copy(src, dst, small_sem.at[i])
        for i, (src, dst) in enumerate([
            (x_hbm, hg.at[g]), (scale_hbm, scale_ref), (shift_hbm, shift_ref),
            (kg_hbm, kg_ref), (qg_hbm, qg_ref), (win_hbm, win_ref)])
    ]
    for copy in smalls:
        copy.start()
    w_copies = [pltpu.make_async_copy(w_hbm.at[j], wq.at[j], w_sem.at[j]) for j in range(3)]
    for j in (1, 2, 0):
        w_copies[j].start()

    def columns(i):
        return wo_hbm.at[:, pl.ds(pl.multiple_of(i * W, W), W)]

    wo_own = pltpu.make_async_copy(columns(g), wo.at[g], own_sem)
    wo_own.start()

    barrier = pltpu.get_barrier_semaphore()
    greeted = [on_head(lax.rem(g + i, NG)) for i in range(1, NG)]
    greeted += [z + (x0 + k,) for z in (z_prev, z_next) for k in range(2)]
    greeted += [(r, y_to, g), (r, y_from, g)]
    for dev in greeted:
        pl.semaphore_signal(barrier, inc=1, device_id=dev, device_id_type=MESH)
    pl.semaphore_wait(barrier, len(greeted))

    half = T // 2

    def ag_copy(slot, part, send, dev):
        piece = hg.at[slot, pl.ds(part * half, half), :]
        return pltpu.make_async_remote_copy(
            src_ref=piece, dst_ref=piece, send_sem=send, recv_sem=ag_r.at[slot, part],
            device_id=on_head(dev), device_id_type=MESH)

    gathers = []

    def gather(slot, part, send, dev):
        copy = ag_copy(slot, part, send, dev)
        copy.start()
        gathers.append(copy)

    def gathered(slot, part):
        ag_copy(slot, part, ag_s.at[0], mate).wait_recv()

    smalls[0].wait()
    for i in range(2):
        gather(g, i, ag_s.at[i], right)
        gather(g, 1 - i, ag_s.at[2 + i], left)
    for part in range(2):
        gather(g, part, ag_s.at[4 + part], mate)
    gathered(left, 0)
    gather(left, 0, agx_s.at[0], right)
    gathered(right, 1)
    gather(right, 1, agx_s.at[1], left)
    gather(left, 0, agf_s.at[0, 0], mate)
    gather(right, 1, agf_s.at[1, 1], mate)
    gathered(left, 1)
    gather(left, 1, agf_s.at[0, 1], mate)
    gathered(right, 0)
    gather(right, 0, agf_s.at[1, 0], mate)
    for part in range(2):
        gathered(peers[2], part)
        gather(peers[2], part, agf_s.at[2, part], mate)
    for dev in [mate] + [dev + 1 - 2 * core for dev in peers]:
        for part in range(2):
            gathered(dev, part)
    for copy in smalls[1:]:
        copy.wait()

    step = 32

    def norm_rows(i, _):
        rows = pl.ds(pl.multiple_of(i * step, step), step)
        parts = [hg[j, rows, :].astype(F32) for j in range(NG)]
        total = parts[0]
        for part in parts[1:]:
            total = total + part
        center = jnp.sum(total, axis=-1, keepdims=True) * (1.0 / D)
        squares = None
        for part in parts:
            off = part - center
            squares = off * off if squares is None else squares + off * off
        spread = jnp.sum(squares, axis=-1, keepdims=True) * (1.0 / D)
        inv = lax.rsqrt(spread + 1e-6)
        for j in range(NG):
            cols = slice(j * W, (j + 1) * W)
            nb[rows, cols] = (
                (parts[j] - center) * inv * (1.0 + scale_ref[:, cols]) + shift_ref[:, cols]
            ).astype(BF16)
        return 0

    lax.fori_loop(0, T // step, norm_rows, 0)

    def kv_copy(src, dst, h, part, send, dev):
        return pltpu.make_async_remote_copy(
            src_ref=kv.at[src, h, part], dst_ref=kv.at[dst, h, part],
            send_sem=send, recv_sem=kv_r.at[dst, h, part],
            device_id=dev, device_id_type=MESH)

    def own_copy(way, h, part):
        first = jnp.where(r == 0, 0, 2) if way == 0 else jnp.where(r == 3, 0, 2)
        slot = first + 3 * jnp.where(core == way, 0, 1)
        to = z_prev if way == 0 else z_next
        return kv_copy(OWN, slot, h, part, kv_s.at[way, h, part], to + (x0 + way,))

    ranks = (r, 3 - r)

    def send_own(h, part):
        for way in range(2):
            @pl.when((h == 0) | (ranks[way] > 0))
            def _():
                own_copy(way, h, part).start()

    def send_later(h):
        for way in range(2):
            @pl.when(ranks[way] == 0)
            def _():
                for part in range(2):
                    own_copy(way, h, part).start()

    def project(j):
        w_copies[j].wait()
        return jnp.dot(nb[...], wq[j], preferred_element_type=F32)

    def head_norm(values, gain):
        mean = jnp.mean(values * values, axis=-1, keepdims=True)
        return (values * lax.rsqrt(mean + 1e-6) * gain).astype(BF16)

    keys = project(1)
    for h in range(NH):
        kv[OWN, h, 0] = head_norm(keys[:, h * HD:(h + 1) * HD], kg_ref[...])
        send_own(h, 0)
    values = project(2)
    for h in range(NH):
        kv[OWN, h, 1] = values[:, h * HD:(h + 1) * HD].astype(BF16)
        send_own(h, 1)

    def q_copy(h, dev):
        return pltpu.make_async_remote_copy(
            src_ref=qs.at[0, h], dst_ref=qs.at[1, h], send_sem=q_s.at[h], recv_sem=q_r.at[h],
            device_id=(r, dev, g), device_id_type=MESH)

    def mk_copy(dev):
        return pltpu.make_async_remote_copy(
            src_ref=mk.at[0], dst_ref=mk.at[1], send_sem=mk_s, recv_sem=mk_r,
            device_id=(r, dev, g), device_id_type=MESH)

    for i in range(9):
        mk[0, i:i + 1, :] = jnp.full((1, HD), win_ref[0, 0, i].astype(F32))

    @pl.when(has_in)
    def _():
        mk_copy(y_from).start()

    queries = project(0)
    for h in range(NH):
        qs[0, h] = head_norm(queries[:, h * HD:(h + 1) * HD], qg_ref[...])

        @pl.when(has_in)
        def _():
            q_copy(h, y_from).start()

    def wo_copy(i):
        dev = lax.rem(g + i, NG)
        return pltpu.make_async_remote_copy(
            src_ref=columns(dev), dst_ref=wo.at[g], send_sem=wo_s.at[i], recv_sem=wo_r.at[g],
            device_id=on_head(dev), device_id_type=MESH)

    for i in range(1, NG):
        wo_copy(i).start()

    m_s[...] = jnp.full_like(m_s, NEG)
    l_s[...] = jnp.zeros_like(l_s)
    acc[...] = jnp.zeros_like(acc)
    block = 128

    def attend(who, slot, h, offset):
        kept = mk[who, pl.ds(offset, 1), :] > 0
        k = kv[slot, h, 0]
        v = kv[slot, h, 1]
        for i in range(T // block):
            rows = slice(i * block, (i + 1) * block)
            s = lax.dot_general(
                qs[who, h, rows, :], k, (((1,), (1,)), ((), ())), preferred_element_type=F32)
            top = jnp.max(s, axis=-1, keepdims=True) * SCALE
            old = m_s[who, h, rows, :]
            new = jnp.maximum(old, jnp.where(kept, top, NEG))
            decay = jnp.exp2(old - new)
            less = jnp.where(kept, new, -NEG)
            p = jnp.exp2(s * SCALE - jnp.concatenate([less] * (T // HD), axis=1))
            m_s[who, h, rows, :] = new
            l_s[who, h, rows, :] = l_s[who, h, rows, :] * decay + jnp.sum(p, axis=-1, keepdims=True)
            acc[who, h, rows, :] = acc[who, h, rows, :] * decay + jnp.dot(
                p.astype(BF16), v, preferred_element_type=F32)

    def own_tile(h, _):
        attend(0, OWN, h, 4)
        return 0

    lax.fori_loop(0, NH, own_tile, 0)

    def arrived(slot, h, part):
        kv_copy(OWN, slot, h, part, kv_s.at[0, h, part], (r, c, mate)).wait_recv()

    def event(at_rank, i):
        first = jnp.where(at_rank < 3, NH, 0)
        crossing = (i >= first) & (i < first + 2 * NH)
        e = jnp.where(crossing, i - first, 0)
        k = lax.rem(e, 2)
        h = jnp.where(crossing, e // 2, i)
        valid = (i >= 0) & (i < first + 2 * NH)
        return valid, crossing, k, jnp.where(valid, h, 0)

    def relay(i, part, other, act):
        valid, crossing, k, h = event(rank, i)
        near = k + 1 >= rank
        slot = jnp.where(crossing, k, 2) + 3 * other
        k_out = jnp.where(crossing, k, 1)

        @pl.when(valid & jnp.where(crossing, rank > 0, rank == 0))
        def _():
            act(kv_copy(slot, k_out + 3 * other, h, part, z_s.at[k_out, other, h, part], onward))

        @pl.when((other == 1) & valid & (near | jnp.logical_not(crossing)))
        def _():
            kind = jnp.where(crossing, k, 2)
            act(kv_copy(slot, MATE + kind, h, part, mate_s.at[kind, h, part], (r, c, mate)))

    def at_copy(slot, h, send, dev):
        return pltpu.make_async_remote_copy(
            src_ref=at.at[slot, h], dst_ref=at.at[slot, h], send_sem=send, recv_sem=at_r.at[slot, h],
            device_id=on_head(dev), device_id_type=MESH)

    def back_copies(h, dev):
        return [
            pltpu.make_async_remote_copy(
                src_ref=buf.at[0, h], dst_ref=buf.at[1, h], send_sem=back_s.at[i, h],
                recv_sem=back_r.at[i, h], device_id=(r, dev, g), device_id_type=MESH)
            for i, buf in enumerate((stats, back))
        ]

    def give_back(h):
        stats[0, h, 0:1, :] = jnp.transpose(m_s[1, h])[0:1, :]
        stats[0, h, 1:2, :] = jnp.transpose(l_s[1, h])[0:1, :]
        back[0, h] = acc[1, h].astype(BF16)
        for copy in back_copies(h, y_to):
            copy.start()

    def finish_head(h):
        @pl.when(has_in)
        def _():
            for copy in back_copies(h, y_from):
                copy.wait_recv()
            m1, l1 = [
                jnp.transpose(jnp.broadcast_to(stats[1, h, i:i + 1, :], (HD, T))) for i in range(2)]
            m0 = m_s[0, h]
            top = jnp.maximum(m0, m1)
            a0, a1 = jnp.exp2(m0 - top), jnp.exp2(m1 - top)
            l_s[0, h] = l_s[0, h] * a0 + l1 * a1
            acc[0, h] = acc[0, h] * a0 + back[1, h].astype(F32) * a1

        at[g, h] = (acc[0, h] / l_s[0, h]).astype(BF16)
        for i, dev in enumerate(peers + [mate]):
            at_copy(g, h, at_s.at[i, h], dev).start()

    def pass_head(h):
        for i, dev in enumerate(peers):
            at_copy(dev, h, at_s.at[i, h], dev).wait_recv()
            at_copy(dev, h, atf_s.at[i, h], mate).start()

    def tick(t, _):
        done = t - LAG - NH - 1

        @pl.when((t == LAG_OWN) & has_out)
        def _():
            mk_copy(y_to).wait_recv()
            for h in range(NH):
                q_copy(h, y_to).wait_recv()

        def turn_of(i, _):
            part, other = i // 2, lax.rem(i, 2)
            valid, crossing, k, h = event(rank, t)

            @pl.when(valid)
            def _():
                arrived(jnp.where(crossing, k, 2) + 3 * other, h, part)
                relay(t, part, other, lambda copy: copy.start())

            ours = lax.rem(i, 2) == 0
            far = i < 2
            at_rank = jnp.where(ours, rank, 3 - rank)
            valid, crossing, k, h = event(at_rank, t - jnp.where(ours, LAG_OWN, LAG))
            near = k + 1 >= at_rank
            downward = jnp.where(ours, core, 1 - core) == 0
            turn = jnp.where(downward, k, 3 - k) - r + 1
            kind = jnp.where(crossing, k, 2)
            slot = jnp.where(ours, kind, MATE + kind)
            side = jnp.where(far, 2 * zh, 2 - 2 * zh)
            offset = jnp.where(crossing, 3 * turn + side, jnp.where(downward, 7, 1))
            needed = valid & jnp.where(crossing, near, True)

            @pl.when(needed & (i == 1))
            def _():
                arrived(slot, h, 0)
                arrived(slot, h, 1)

            @pl.when(needed & jnp.where(far, crossing & has_out, True))
            def _():
                attend(jnp.where(far, 1, 0), slot, h, offset)

            @pl.when((i == 1) & (done >= 0) & (lax.rem(done, 2) == 0) & has_out)
            def _():
                give_back(done // 2)

            return 0

        lax.fori_loop(0, 4, turn_of, 0)

        @pl.when(t < NH - 1)
        def _():
            send_later(t + 1)

        back_in = done - LAG_BACK

        @pl.when((back_in >= 0) & (lax.rem(back_in, 2) == 0))
        def _():
            ready = back_in // 2
            finish_head(ready)

            @pl.when(ready > 0)
            def _():
                pass_head(ready - 1)

        return 0

    lax.fori_loop(0, EVENTS + LAG + LAG_BACK, tick, 0)
    pass_head(NH - 1)
    for h in range(NH):
        at_copy(mate, h, at_s.at[3, h], mate).wait_recv()
        for i, dev in enumerate(peers):
            at_copy(dev + 1 - 2 * core, h, atf_s.at[i, h], mate).wait_recv()
    wo_own.wait()
    for i in range(1, NG):
        src = lax.rem(g + i, NG)
        pltpu.make_async_remote_copy(
            src_ref=columns(src), dst_ref=wo.at[src], send_sem=wo_s.at[i], recv_sem=wo_r.at[src],
            device_id=on_head(src), device_id_type=MESH).wait_recv()


    def group(i, total):
        a = jnp.concatenate([at[i, h] for h in range(NH)], axis=1)
        part = jnp.dot(a, wo[i], preferred_element_type=F32)
        return total + part.astype(BF16).astype(F32)

    proj = lax.fori_loop(0, NG, group, jnp.zeros((T, W), F32))
    out_ref[...] = proj

    for copy in gathers:
        copy.wait_send()
    for i in range(1, NG):
        wo_copy(i).wait_send()
    for h in range(NH):
        for i, dev in enumerate(peers + [mate]):
            at_copy(g, h, at_s.at[i, h], dev).wait_send()
        for i, dev in enumerate(peers):
            at_copy(dev, h, atf_s.at[i, h], mate).wait_send()

    def sent(i, _):
        for part in range(2):
            for other in range(2):
                relay(i, part, other, lambda copy: copy.wait_send())
        return 0

    lax.fori_loop(0, EVENTS, sent, 0)

    @pl.when(has_in)
    def _():
        mk_copy(y_from).wait_send()
        for h in range(NH):
            q_copy(h, y_from).wait_send()

    @pl.when(has_out)
    def _():
        for h in range(NH):
            for copy in back_copies(h, y_to):
                copy.wait_send()

    for way in range(2):
        for h in range(NH):
            for part in range(2):
                own_copy(way, h, part).wait_send()


def on_device(
    hidden_in, mod_shift, mod_scale, mod_gate, w_qkv, query_gain, key_gain, w_out, window
):
    vmem = pl.BlockSpec(memory_space=pltpu.VMEM)
    hbm = pl.BlockSpec(memory_space=pltpu.HBM)
    dma = pltpu.SemaphoreType.DMA
    proj = pl.pallas_call(
        kernel,
        out_shape=jax.ShapeDtypeStruct((T, W), F32),
        in_specs=[hbm] * 8,
        out_specs=vmem,
        scratch_shapes=[
            pltpu.VMEM((1, D), F32),
            pltpu.VMEM((1, D), F32),
            pltpu.VMEM((1, HD), F32),
            pltpu.VMEM((1, HD), F32),
            pltpu.SMEM((1, 1, 9), jnp.int32),
            dma((6,)),
            pltpu.VMEM((NG, T, W), BF16),
            pltpu.VMEM((T, D), BF16),
            pltpu.VMEM((3, D, W), BF16),
            pltpu.VMEM((SLOTS, NH, 2, T, HD), BF16),
            pltpu.VMEM((2, NH, T, HD), BF16),
            pltpu.VMEM((2, NH, T, HD), F32),
            pltpu.VMEM((2, NH, T, HD), F32),
            pltpu.VMEM((2, NH, T, HD), F32),
            pltpu.VMEM((NG, W, W), BF16),
            pltpu.VMEM((NG, NH, T, HD), BF16),
            pltpu.VMEM((2, 16, HD), F32),
            pltpu.VMEM((2, NH, T, HD), BF16),
            pltpu.VMEM((2, NH, 8, T), F32),
            dma((3,)), dma, dma((6,)), dma((2,)), dma((3, 2)), dma((NG, 2)),
            dma((2, NH, 2)), dma((2, 2, NH, 2)), dma((3, NH, 2)), dma((SLOTS, NH, 2)),
            dma((NH,)), dma((NH,)), dma, dma, dma((2, NH)), dma((2, NH)),
            dma((NG,)), dma((NG,)), dma((4, NH)), dma((3, NH)), dma((NG, NH)),
        ],
        compiler_params=pltpu.CompilerParams(
            collective_id=0, has_side_effects=True, vmem_limit_bytes=64 * 1024 * 1024),
        cost_estimate=pl.CostEstimate(
            flops=6_000_000_000, bytes_accessed=10_000_000, transcendentals=4_000_000),
        name="tile_attention",
    )(
        hidden_in.reshape(T, W),
        mod_shift.reshape(1, D),
        mod_scale.reshape(1, D),
        jnp.transpose(w_qkv, (1, 0, 2)),
        query_gain.reshape(1, HD),
        key_gain.reshape(1, HD),
        w_out,
        window,
    )
    proj = proj.reshape(hidden_in.shape)
    return (hidden_in.astype(F32) + mod_gate * proj).astype(BF16)


def solution(mesh):
    in_specs = (
        P("row", "col", None, "head"),
        P(),
        P(),
        P("head"),
        P(None, None, "head"),
        P(),
        P(),
        P("head", None),
        P("row", "col", None),
    )
    out_specs = P("row", "col", None, "head")
    return jax.shard_map(
        on_device, mesh=mesh, in_specs=in_specs, out_specs=out_specs, check_vma=False
    )
```

```python
import functools
import math

import jax
import jax.numpy as jnp
from jax import lax
from jax.experimental import pallas as pl
from jax.experimental.pallas import tpu as pltpu
from jax.sharding import PartitionSpec as P

MESH = pl.DeviceIdType.MESH
F32 = jnp.float32
BF16 = jnp.bfloat16
HD = 128
NH = 3
NG = 8
T = 384
W = NH * HD
D = NG * W
ROWS = 4
OWN, MATE = 6, 7
SLOTS = 10
SCALE = math.log2(math.e) / math.sqrt(HD)
NEG = -1e30
EVENTS = 9
LAG_OWN, LAG = 1, 2
LAG_BACK = 1


def kernel(
    x_hbm, shift_hbm, scale_hbm, gate_hbm, w_hbm, qg_hbm, kg_hbm, wo_hbm, win_hbm, out_ref,
    gate_ref, proj,
    shift_ref, scale_ref, qg_ref, kg_ref, win_ref, small_sem, hg, nb, wq, kv, qs, acc, m_s, l_s, wo, at, mk, back, stats,
    w_sem, own_sem, ag_s, agx_s, agf_s, ag_r, kv_s, z_s, mate_s, kv_r, q_s, q_r, mk_s, mk_r, back_s, back_r, wo_s, wo_r, at_s, atf_s, at_r,
):
    r = lax.axis_index("row")
    c = lax.axis_index("col")
    g = lax.axis_index("head")
    y, zh = c // 2, c % 2
    core = g % 2
    mate = g + 1 - 2 * core
    right, left = lax.rem(g + 2, NG), lax.rem(g + 6, NG)
    peers = [lax.rem(g + 2, NG), lax.rem(g + 6, NG), lax.rem(g + 4, NG)]
    x0 = g - core
    z_next = (jnp.where(r < 3, r + 1, 0), jnp.where(r < 3, c, c + 1 - 2 * zh))
    z_prev = (jnp.where(r > 0, r - 1, 3), jnp.where(r > 0, c, c + 1 - 2 * zh))
    rank = jnp.where(core == 0, r, 3 - r)
    onward = (
        jnp.where(core == 0, z_prev[0], z_next[0]), jnp.where(core == 0, z_prev[1], z_next[1]), g)
    y_to = lax.rem(jnp.where(zh == 0, c + 2, c + 6), 8)
    y_from = lax.rem(jnp.where(zh == 0, c + 6, c + 2), 8)
    has_out = jnp.where(zh == 0, y < 3, y > 0)
    has_in = jnp.where(zh == 0, y > 0, y < 3)

    def on_head(i):
        return (r, c, i)

    smalls = [
        pltpu.make_async_copy(src, dst, small_sem.at[i])
        for i, (src, dst) in enumerate([
            (x_hbm, hg.at[g]), (scale_hbm, scale_ref), (shift_hbm, shift_ref),
            (kg_hbm, kg_ref), (qg_hbm, qg_ref), (win_hbm, win_ref), (gate_hbm, gate_ref.at[0])])
    ]
    for copy in smalls:
        copy.start()
    w_copies = [pltpu.make_async_copy(w_hbm.at[j], wq.at[j], w_sem.at[j]) for j in range(3)]
    for j in (1, 2, 0):
        w_copies[j].start()

    def columns(i):
        return wo_hbm.at[:, pl.ds(pl.multiple_of(i * W, W), W)]

    wo_own = pltpu.make_async_copy(columns(g), wo.at[g], own_sem)
    wo_own.start()

    barrier = pltpu.get_barrier_semaphore()
    greeted = [on_head(lax.rem(g + i, NG)) for i in range(1, NG)]
    greeted += [z + (x0 + k,) for z in (z_prev, z_next) for k in range(2)]
    greeted += [(r, y_to, g), (r, y_from, g)]
    for dev in greeted:
        pl.semaphore_signal(barrier, inc=1, device_id=dev, device_id_type=MESH)
    pl.semaphore_wait(barrier, len(greeted))

    half = T // 2

    def ag_copy(slot, part, send, dev):
        piece = hg.at[slot, pl.ds(part * half, half), :]
        return pltpu.make_async_remote_copy(
            src_ref=piece, dst_ref=piece, send_sem=send, recv_sem=ag_r.at[slot, part],
            device_id=on_head(dev), device_id_type=MESH)

    gathers = []

    def gather(slot, part, send, dev):
        copy = ag_copy(slot, part, send, dev)
        copy.start()
        gathers.append(copy)

    def gathered(slot, part):
        ag_copy(slot, part, ag_s.at[0], mate).wait_recv()

    smalls[0].wait()
    for i in range(2):
        gather(g, i, ag_s.at[i], right)
        gather(g, 1 - i, ag_s.at[2 + i], left)
    for part in range(2):
        gather(g, part, ag_s.at[4 + part], mate)
    gathered(left, 0)
    gather(left, 0, agx_s.at[0], right)
    gathered(right, 1)
    gather(right, 1, agx_s.at[1], left)
    gather(left, 0, agf_s.at[0, 0], mate)
    gather(right, 1, agf_s.at[1, 1], mate)
    gathered(left, 1)
    gather(left, 1, agf_s.at[0, 1], mate)
    gathered(right, 0)
    gather(right, 0, agf_s.at[1, 0], mate)
    for part in range(2):
        gathered(peers[2], part)
        gather(peers[2], part, agf_s.at[2, part], mate)
    for dev in [mate] + [dev + 1 - 2 * core for dev in peers]:
        for part in range(2):
            gathered(dev, part)
    for copy in smalls[1:]:
        copy.wait()

    step = 32

    def norm_rows(i, _):
        rows = pl.ds(pl.multiple_of(i * step, step), step)
        parts = [hg[j, rows, :].astype(F32) for j in range(NG)]
        total = parts[0]
        for part in parts[1:]:
            total = total + part
        center = jnp.sum(total, axis=-1, keepdims=True) * (1.0 / D)
        squares = None
        for part in parts:
            off = part - center
            squares = off * off if squares is None else squares + off * off
        spread = jnp.sum(squares, axis=-1, keepdims=True) * (1.0 / D)
        inv = lax.rsqrt(spread + 1e-6)
        for j in range(NG):
            cols = slice(j * W, (j + 1) * W)
            nb[rows, cols] = (
                (parts[j] - center) * inv * (1.0 + scale_ref[:, cols]) + shift_ref[:, cols]
            ).astype(BF16)
        return 0

    lax.fori_loop(0, T // step, norm_rows, 0)

    def kv_copy(src, dst, h, part, send, dev):
        return pltpu.make_async_remote_copy(
            src_ref=kv.at[src, h, part], dst_ref=kv.at[dst, h, part],
            send_sem=send, recv_sem=kv_r.at[dst, h, part],
            device_id=dev, device_id_type=MESH)

    def own_copy(way, h, part):
        first = jnp.where(r == 0, 0, 2) if way == 0 else jnp.where(r == 3, 0, 2)
        slot = first + 3 * jnp.where(core == way, 0, 1)
        to = z_prev if way == 0 else z_next
        return kv_copy(OWN, slot, h, part, kv_s.at[way, h, part], to + (x0 + way,))

    ranks = (r, 3 - r)

    def send_own(h, part):
        for way in range(2):
            @pl.when((h == 0) | (ranks[way] > 0))
            def _():
                own_copy(way, h, part).start()

    def send_later(h):
        for way in range(2):
            @pl.when(ranks[way] == 0)
            def _():
                for part in range(2):
                    own_copy(way, h, part).start()

    def project(j):
        w_copies[j].wait()
        return jnp.dot(nb[...], wq[j], preferred_element_type=F32)

    def head_norm(values, gain):
        mean = jnp.mean(values * values, axis=-1, keepdims=True)
        return (values * lax.rsqrt(mean + 1e-6) * gain).astype(BF16)

    keys = project(1)
    for h in range(NH):
        kv[OWN, h, 0] = head_norm(keys[:, h * HD:(h + 1) * HD], kg_ref[...])
        send_own(h, 0)
    values = project(2)
    for h in range(NH):
        kv[OWN, h, 1] = values[:, h * HD:(h + 1) * HD].astype(BF16)
        send_own(h, 1)

    def q_copy(h, dev):
        return pltpu.make_async_remote_copy(
            src_ref=qs.at[0, h], dst_ref=qs.at[1, h], send_sem=q_s.at[h], recv_sem=q_r.at[h],
            device_id=(r, dev, g), device_id_type=MESH)

    def mk_copy(dev):
        return pltpu.make_async_remote_copy(
            src_ref=mk.at[0], dst_ref=mk.at[1], send_sem=mk_s, recv_sem=mk_r,
            device_id=(r, dev, g), device_id_type=MESH)

    for i in range(9):
        mk[0, i:i + 1, :] = jnp.full((1, HD), win_ref[0, 0, i].astype(F32))

    @pl.when(has_in)
    def _():
        mk_copy(y_from).start()

    queries = project(0)
    for h in range(NH):
        qs[0, h] = head_norm(queries[:, h * HD:(h + 1) * HD], qg_ref[...])

        @pl.when(has_in)
        def _():
            q_copy(h, y_from).start()

    def wo_copy(i):
        dev = lax.rem(g + i, NG)
        return pltpu.make_async_remote_copy(
            src_ref=columns(dev), dst_ref=wo.at[g], send_sem=wo_s.at[i], recv_sem=wo_r.at[g],
            device_id=on_head(dev), device_id_type=MESH)

    for i in range(1, NG):
        wo_copy(i).start()

    m_s[...] = jnp.full_like(m_s, NEG)
    l_s[...] = jnp.zeros_like(l_s)
    acc[...] = jnp.zeros_like(acc)
    block = 128

    def attend(who, slot, h, offset):
        kept = mk[who, pl.ds(offset, 1), :] > 0
        k = kv[slot, h, 0]
        v = kv[slot, h, 1]
        for i in range(T // block):
            rows = slice(i * block, (i + 1) * block)
            s = lax.dot_general(
                qs[who, h, rows, :], k, (((1,), (1,)), ((), ())), preferred_element_type=F32)
            top = jnp.max(s, axis=-1, keepdims=True) * SCALE
            old = m_s[who, h, rows, :]
            new = jnp.maximum(old, jnp.where(kept, top, NEG))
            decay = jnp.exp2(old - new)
            less = jnp.where(kept, new, -NEG)
            p = jnp.exp2(s * SCALE - jnp.concatenate([less] * (T // HD), axis=1))
            m_s[who, h, rows, :] = new
            l_s[who, h, rows, :] = l_s[who, h, rows, :] * decay + jnp.sum(p, axis=-1, keepdims=True)
            acc[who, h, rows, :] = acc[who, h, rows, :] * decay + jnp.dot(
                p.astype(BF16), v, preferred_element_type=F32)

    def own_tile(h, _):
        attend(0, OWN, h, 4)
        return 0

    lax.fori_loop(0, NH, own_tile, 0)

    def arrived(slot, h, part):
        kv_copy(OWN, slot, h, part, kv_s.at[0, h, part], (r, c, mate)).wait_recv()

    def event(at_rank, i):
        first = jnp.where(at_rank < 3, NH, 0)
        crossing = (i >= first) & (i < first + 2 * NH)
        e = jnp.where(crossing, i - first, 0)
        k = lax.rem(e, 2)
        h = jnp.where(crossing, e // 2, i)
        valid = (i >= 0) & (i < first + 2 * NH)
        return valid, crossing, k, jnp.where(valid, h, 0)

    def relay(i, part, other, act):
        valid, crossing, k, h = event(rank, i)
        near = k + 1 >= rank
        slot = jnp.where(crossing, k, 2) + 3 * other
        k_out = jnp.where(crossing, k, 1)

        @pl.when(valid & jnp.where(crossing, rank > 0, rank == 0))
        def _():
            act(kv_copy(slot, k_out + 3 * other, h, part, z_s.at[k_out, other, h, part], onward))

        @pl.when((other == 1) & valid & (near | jnp.logical_not(crossing)))
        def _():
            kind = jnp.where(crossing, k, 2)
            act(kv_copy(slot, MATE + kind, h, part, mate_s.at[kind, h, part], (r, c, mate)))

    def at_copy(slot, h, send, dev):
        return pltpu.make_async_remote_copy(
            src_ref=at.at[slot, h], dst_ref=at.at[slot, h], send_sem=send, recv_sem=at_r.at[slot, h],
            device_id=on_head(dev), device_id_type=MESH)

    def back_copies(h, dev):
        return [
            pltpu.make_async_remote_copy(
                src_ref=buf.at[0, h], dst_ref=buf.at[1, h], send_sem=back_s.at[i, h],
                recv_sem=back_r.at[i, h], device_id=(r, dev, g), device_id_type=MESH)
            for i, buf in enumerate((stats, back))
        ]

    def give_back(h):
        stats[0, h, 0:1, :] = jnp.transpose(m_s[1, h])[0:1, :]
        stats[0, h, 1:2, :] = jnp.transpose(l_s[1, h])[0:1, :]
        back[0, h] = acc[1, h].astype(BF16)
        for copy in back_copies(h, y_to):
            copy.start()

    def finish_head(h):
        @pl.when(has_in)
        def _():
            for copy in back_copies(h, y_from):
                copy.wait_recv()
            m1, l1 = [
                jnp.transpose(jnp.broadcast_to(stats[1, h, i:i + 1, :], (HD, T))) for i in range(2)]
            m0 = m_s[0, h]
            top = jnp.maximum(m0, m1)
            a0, a1 = jnp.exp2(m0 - top), jnp.exp2(m1 - top)
            l_s[0, h] = l_s[0, h] * a0 + l1 * a1
            acc[0, h] = acc[0, h] * a0 + back[1, h].astype(F32) * a1

        at[g, h] = (acc[0, h] / l_s[0, h]).astype(BF16)
        for i, dev in enumerate(peers + [mate]):
            at_copy(g, h, at_s.at[i, h], dev).start()

    def pass_head(h):
        for i, dev in enumerate(peers):
            at_copy(dev, h, at_s.at[i, h], dev).wait_recv()
            at_copy(dev, h, atf_s.at[i, h], mate).start()

    def tick(t, _):
        done = t - LAG - NH - 1

        @pl.when((t == LAG_OWN) & has_out)
        def _():
            mk_copy(y_to).wait_recv()
            for h in range(NH):
                q_copy(h, y_to).wait_recv()

        def turn_of(i, _):
            part, other = i // 2, lax.rem(i, 2)
            valid, crossing, k, h = event(rank, t)

            @pl.when(valid)
            def _():
                arrived(jnp.where(crossing, k, 2) + 3 * other, h, part)
                relay(t, part, other, lambda copy: copy.start())

            ours = lax.rem(i, 2) == 0
            far = i < 2
            at_rank = jnp.where(ours, rank, 3 - rank)
            valid, crossing, k, h = event(at_rank, t - jnp.where(ours, LAG_OWN, LAG))
            near = k + 1 >= at_rank
            downward = jnp.where(ours, core, 1 - core) == 0
            turn = jnp.where(downward, k, 3 - k) - r + 1
            kind = jnp.where(crossing, k, 2)
            slot = jnp.where(ours, kind, MATE + kind)
            side = jnp.where(far, 2 * zh, 2 - 2 * zh)
            offset = jnp.where(crossing, 3 * turn + side, jnp.where(downward, 7, 1))
            needed = valid & jnp.where(crossing, near, True)

            @pl.when(needed & (i == 1))
            def _():
                arrived(slot, h, 0)
                arrived(slot, h, 1)

            @pl.when(needed & jnp.where(far, crossing & has_out, True))
            def _():
                attend(jnp.where(far, 1, 0), slot, h, offset)

            @pl.when((i == 1) & (done >= 0) & (lax.rem(done, 2) == 0) & has_out)
            def _():
                give_back(done // 2)

            return 0

        lax.fori_loop(0, 4, turn_of, 0)

        @pl.when(t < NH - 1)
        def _():
            send_later(t + 1)

        back_in = done - LAG_BACK

        @pl.when((back_in >= 0) & (lax.rem(back_in, 2) == 0))
        def _():
            ready = back_in // 2
            finish_head(ready)

            @pl.when(ready > 0)
            def _():
                pass_head(ready - 1)

        return 0

    lax.fori_loop(0, EVENTS + LAG + LAG_BACK, tick, 0)
    wo_own.wait()
    for i in range(1, NG):
        src = lax.rem(g + i, NG)
        pltpu.make_async_remote_copy(
            src_ref=columns(src), dst_ref=wo.at[src], send_sem=wo_s.at[i], recv_sem=wo_r.at[src],
            device_id=on_head(src), device_id_type=MESH).wait_recv()

    def group(i):
        a = jnp.concatenate([at[i, h] for h in range(NH)], axis=1)
        part = jnp.dot(a, wo[i], preferred_element_type=F32)
        return part.astype(BF16).astype(F32)

    last = NH - 1
    proj[...] = group(g)
    for i, dev in enumerate(peers):
        at_copy(dev, last, at_s.at[i, last], dev).wait_recv()
        at_copy(dev, last, atf_s.at[i, last], mate).start()
        if i < 2:
            proj[...] += group(dev)

    def from_mate(i, _):
        src = mate
        for n, dev in enumerate(peers):
            src = jnp.where(i == n + 1, dev + 1 - 2 * core, src)

        for h in range(NH):
            at_copy(src, h, at_s.at[3, h], mate).wait_recv()
        proj[...] += group(src)
        return 0

    from_mate(0, 0)
    proj[...] += group(peers[2])
    lax.fori_loop(1, 4, from_mate, 0)
    out_ref[...] = (hg[g].astype(F32) + gate_ref[...] * proj[...]).astype(BF16)

    for copy in gathers:
        copy.wait_send()
    for i in range(1, NG):
        wo_copy(i).wait_send()
    for h in range(NH):
        for i, dev in enumerate(peers + [mate]):
            at_copy(g, h, at_s.at[i, h], dev).wait_send()
        for i, dev in enumerate(peers):
            at_copy(dev, h, atf_s.at[i, h], mate).wait_send()

    def sent(i, _):
        for part in range(2):
            for other in range(2):
                relay(i, part, other, lambda copy: copy.wait_send())
        return 0

    lax.fori_loop(0, EVENTS, sent, 0)

    @pl.when(has_in)
    def _():
        mk_copy(y_from).wait_send()
        for h in range(NH):
            q_copy(h, y_from).wait_send()

    @pl.when(has_out)
    def _():
        for h in range(NH):
            for copy in back_copies(h, y_to):
                copy.wait_send()

    for way in range(2):
        for h in range(NH):
            for part in range(2):
                own_copy(way, h, part).wait_send()


def on_device(
    hidden_in, mod_shift, mod_scale, mod_gate, w_qkv, query_gain, key_gain, w_out, window
):
    vmem = pl.BlockSpec(memory_space=pltpu.VMEM)
    hbm = pl.BlockSpec(memory_space=pltpu.HBM)
    dma = pltpu.SemaphoreType.DMA
    out = pl.pallas_call(
        kernel,
        out_shape=jax.ShapeDtypeStruct((T, W), BF16),
        in_specs=[hbm] * 9,
        out_specs=vmem,
        scratch_shapes=[
            pltpu.VMEM((1, W), F32),
            pltpu.VMEM((T, W), F32),
            pltpu.VMEM((1, D), F32),
            pltpu.VMEM((1, D), F32),
            pltpu.VMEM((1, HD), F32),
            pltpu.VMEM((1, HD), F32),
            pltpu.SMEM((1, 1, 9), jnp.int32),
            dma((7,)),
            pltpu.VMEM((NG, T, W), BF16),
            pltpu.VMEM((T, D), BF16),
            pltpu.VMEM((3, D, W), BF16),
            pltpu.VMEM((SLOTS, NH, 2, T, HD), BF16),
            pltpu.VMEM((2, NH, T, HD), BF16),
            pltpu.VMEM((2, NH, T, HD), F32),
            pltpu.VMEM((2, NH, T, HD), F32),
            pltpu.VMEM((2, NH, T, HD), F32),
            pltpu.VMEM((NG, W, W), BF16),
            pltpu.VMEM((NG, NH, T, HD), BF16),
            pltpu.VMEM((2, 16, HD), F32),
            pltpu.VMEM((2, NH, T, HD), BF16),
            pltpu.VMEM((2, NH, 8, T), F32),
            dma((3,)), dma, dma((6,)), dma((2,)), dma((3, 2)), dma((NG, 2)),
            dma((2, NH, 2)), dma((2, 2, NH, 2)), dma((3, NH, 2)), dma((SLOTS, NH, 2)),
            dma((NH,)), dma((NH,)), dma, dma, dma((2, NH)), dma((2, NH)),
            dma((NG,)), dma((NG,)), dma((4, NH)), dma((3, NH)), dma((NG, NH)),
        ],
        compiler_params=pltpu.CompilerParams(
            collective_id=0, has_side_effects=True, vmem_limit_bytes=64 * 1024 * 1024),
        cost_estimate=pl.CostEstimate(
            flops=6_000_000_000, bytes_accessed=10_000_000, transcendentals=4_000_000),
        name="tile_attention",
    )(
        hidden_in.reshape(T, W),
        mod_shift.reshape(1, D),
        mod_scale.reshape(1, D),
        mod_gate,
        jnp.transpose(w_qkv, (1, 0, 2)),
        query_gain.reshape(1, HD),
        key_gain.reshape(1, HD),
        w_out,
        window,
    )
    return out.reshape(hidden_in.shape)


def solution(mesh):
    in_specs = (
        P("row", "col", None, "head"),
        P(),
        P(),
        P("head"),
        P(None, None, "head"),
        P(),
        P(),
        P("head", None),
        P("row", "col", None),
    )
    out_specs = P("row", "col", None, "head")
    return jax.shard_map(
        on_device, mesh=mesh, in_specs=in_specs, out_specs=out_specs, check_vma=False
    )
```

```python
import functools
import math

import jax
import jax.numpy as jnp
from jax import lax
from jax.experimental import pallas as pl
from jax.experimental.pallas import tpu as pltpu
from jax.sharding import PartitionSpec as P

MESH = pl.DeviceIdType.MESH
F32 = jnp.float32
BF16 = jnp.bfloat16
HD = 128
NH = 3
NG = 8
T = 384
W = NH * HD
D = NG * W
ROWS = 4
OWN, MATE = 6, 7
SLOTS = 10
SCALE = math.log2(math.e) / math.sqrt(HD)
NEG = -1e30
EVENTS = 9
LAG_OWN, LAG = 1, 2
LAG_BACK = 1


def kernel(
    x_hbm, shift_hbm, scale_hbm, gate_hbm, w_hbm, qg_hbm, kg_hbm, wo_hbm, win_hbm, out_ref,
    gate_ref, proj,
    shift_ref, scale_ref, qg_ref, kg_ref, win_ref, small_sem, hg, nb, wq, kv, qs, acc, m_s, l_s, wo, at, mk, back, stats,
    w_sem, own_sem, ag_s, agx_s, agf_s, ag_r, kv_s, z_s, mate_s, kv_r, q_s, q_r, mk_s, mk_r, back_s, back_r, wo_s, wo_r, at_s, atf_s, at_r,
):
    r = lax.axis_index("row")
    c = lax.axis_index("col")
    g = lax.axis_index("head")
    y, zh = c // 2, c % 2
    core = g % 2
    mate = g + 1 - 2 * core
    right, left = lax.rem(g + 2, NG), lax.rem(g + 6, NG)
    peers = [lax.rem(g + 2, NG), lax.rem(g + 6, NG), lax.rem(g + 4, NG)]
    x0 = g - core
    z_next = (jnp.where(r < 3, r + 1, 0), jnp.where(r < 3, c, c + 1 - 2 * zh))
    z_prev = (jnp.where(r > 0, r - 1, 3), jnp.where(r > 0, c, c + 1 - 2 * zh))
    rank = jnp.where(core == 0, r, 3 - r)
    onward = (
        jnp.where(core == 0, z_prev[0], z_next[0]), jnp.where(core == 0, z_prev[1], z_next[1]), g)
    y_to = lax.rem(jnp.where(zh == 0, c + 2, c + 6), 8)
    y_from = lax.rem(jnp.where(zh == 0, c + 6, c + 2), 8)
    has_out = jnp.where(zh == 0, y < 3, y > 0)
    has_in = jnp.where(zh == 0, y > 0, y < 3)

    def on_head(i):
        return (r, c, i)

    smalls = [
        pltpu.make_async_copy(src, dst, small_sem.at[i])
        for i, (src, dst) in enumerate([
            (x_hbm, hg.at[g]), (scale_hbm, scale_ref), (shift_hbm, shift_ref),
            (kg_hbm, kg_ref), (qg_hbm, qg_ref), (win_hbm, win_ref), (gate_hbm, gate_ref.at[0])])
    ]
    for copy in smalls:
        copy.start()
    w_copies = [pltpu.make_async_copy(w_hbm.at[j], wq.at[j], w_sem.at[j]) for j in range(3)]
    for j in (1, 2, 0):
        w_copies[j].start()

    def columns(i):
        return wo_hbm.at[:, pl.ds(pl.multiple_of(i * W, W), W)]

    wo_own = pltpu.make_async_copy(columns(g), wo.at[g], own_sem)
    wo_own.start()

    barrier = pltpu.get_barrier_semaphore()
    greeted = [on_head(lax.rem(g + i, NG)) for i in range(1, NG)]
    greeted += [z + (x0 + k,) for z in (z_prev, z_next) for k in range(2)]
    greeted += [(r, y_to, g), (r, y_from, g)]
    for dev in greeted:
        pl.semaphore_signal(barrier, inc=1, device_id=dev, device_id_type=MESH)
    pl.semaphore_wait(barrier, len(greeted))

    half = T // 2

    def ag_copy(slot, part, send, dev):
        piece = hg.at[slot, pl.ds(part * half, half), :]
        return pltpu.make_async_remote_copy(
            src_ref=piece, dst_ref=piece, send_sem=send, recv_sem=ag_r.at[slot, part],
            device_id=on_head(dev), device_id_type=MESH)

    gathers = []

    def gather(slot, part, send, dev):
        copy = ag_copy(slot, part, send, dev)
        copy.start()
        gathers.append(copy)

    def gathered(slot, part):
        ag_copy(slot, part, ag_s.at[0], mate).wait_recv()

    smalls[0].wait()
    for i in range(2):
        gather(g, i, ag_s.at[i], right)
        gather(g, 1 - i, ag_s.at[2 + i], left)
    for part in range(2):
        gather(g, part, ag_s.at[4 + part], mate)
    gathered(left, 0)
    gather(left, 0, agx_s.at[0], right)
    gathered(right, 1)
    gather(right, 1, agx_s.at[1], left)
    gather(left, 0, agf_s.at[0, 0], mate)
    gather(right, 1, agf_s.at[1, 1], mate)
    gathered(left, 1)
    gather(left, 1, agf_s.at[0, 1], mate)
    gathered(right, 0)
    gather(right, 0, agf_s.at[1, 0], mate)
    for part in range(2):
        gathered(peers[2], part)
        gather(peers[2], part, agf_s.at[2, part], mate)
    for dev in [mate] + [dev + 1 - 2 * core for dev in peers]:
        for part in range(2):
            gathered(dev, part)
    for copy in smalls[1:]:
        copy.wait()

    step = 32

    def norm_rows(i, _):
        rows = pl.ds(pl.multiple_of(i * step, step), step)
        parts = [hg[j, rows, :].astype(F32) for j in range(NG)]
        total = parts[0]
        for part in parts[1:]:
            total = total + part
        center = jnp.sum(total, axis=-1, keepdims=True) * (1.0 / D)
        squares = None
        for part in parts:
            off = part - center
            squares = off * off if squares is None else squares + off * off
        spread = jnp.sum(squares, axis=-1, keepdims=True) * (1.0 / D)
        inv = lax.rsqrt(spread + 1e-6)
        for j in range(NG):
            cols = slice(j * W, (j + 1) * W)
            nb[rows, cols] = (
                (parts[j] - center) * inv * (1.0 + scale_ref[:, cols]) + shift_ref[:, cols]
            ).astype(BF16)
        return 0

    lax.fori_loop(0, T // step, norm_rows, 0, unroll=2)

    def kv_copy(src, dst, h, part, send, dev):
        return pltpu.make_async_remote_copy(
            src_ref=kv.at[src, h, part], dst_ref=kv.at[dst, h, part],
            send_sem=send, recv_sem=kv_r.at[dst, h, part],
            device_id=dev, device_id_type=MESH)

    def own_copy(way, h, part):
        first = jnp.where(r == 0, 0, 2) if way == 0 else jnp.where(r == 3, 0, 2)
        slot = first + 3 * jnp.where(core == way, 0, 1)
        to = z_prev if way == 0 else z_next
        return kv_copy(OWN, slot, h, part, kv_s.at[way, h, part], to + (x0 + way,))

    ranks = (r, 3 - r)

    def send_own(h, part):
        for way in range(2):
            @pl.when((h == 0) | (ranks[way] > 0))
            def _():
                own_copy(way, h, part).start()

    def send_later(h):
        for way in range(2):
            @pl.when(ranks[way] == 0)
            def _():
                for part in range(2):
                    own_copy(way, h, part).start()

    def project(j):
        w_copies[j].wait()
        return jnp.dot(nb[...], wq[j], preferred_element_type=F32)

    def head_norm(values, gain):
        mean = jnp.mean(values * values, axis=-1, keepdims=True)
        return (values * lax.rsqrt(mean + 1e-6) * gain).astype(BF16)

    keys = project(1)
    for h in range(NH):
        kv[OWN, h, 0] = head_norm(keys[:, h * HD:(h + 1) * HD], kg_ref[...])
        send_own(h, 0)
    values = project(2)
    for h in range(NH):
        kv[OWN, h, 1] = values[:, h * HD:(h + 1) * HD].astype(BF16)
        send_own(h, 1)

    def q_copy(h, dev):
        return pltpu.make_async_remote_copy(
            src_ref=qs.at[0, h], dst_ref=qs.at[1, h], send_sem=q_s.at[h], recv_sem=q_r.at[h],
            device_id=(r, dev, g), device_id_type=MESH)

    def mk_copy(dev):
        return pltpu.make_async_remote_copy(
            src_ref=mk.at[0], dst_ref=mk.at[1], send_sem=mk_s, recv_sem=mk_r,
            device_id=(r, dev, g), device_id_type=MESH)

    for i in range(9):
        mk[0, i:i + 1, :] = jnp.full((1, HD), win_ref[0, 0, i].astype(F32))

    @pl.when(has_in)
    def _():
        mk_copy(y_from).start()

    queries = project(0)
    for h in range(NH):
        qs[0, h] = head_norm(queries[:, h * HD:(h + 1) * HD], qg_ref[...])

        @pl.when(has_in)
        def _():
            q_copy(h, y_from).start()

    def wo_copy(i):
        dev = lax.rem(g + i, NG)
        return pltpu.make_async_remote_copy(
            src_ref=columns(dev), dst_ref=wo.at[g], send_sem=wo_s.at[i], recv_sem=wo_r.at[g],
            device_id=on_head(dev), device_id_type=MESH)

    for i in range(1, NG):
        wo_copy(i).start()

    m_s[...] = jnp.full_like(m_s, NEG)
    l_s[...] = jnp.zeros_like(l_s)
    acc[...] = jnp.zeros_like(acc)
    block = 384

    def attend(who, slot, h, offset):
        kept = mk[who, pl.ds(offset, 1), :] > 0
        k = kv[slot, h, 0]
        v = kv[slot, h, 1]
        for i in range(T // block):
            rows = slice(i * block, (i + 1) * block)
            s = lax.dot_general(
                qs[who, h, rows, :], k, (((1,), (1,)), ((), ())), preferred_element_type=F32)
            top = jnp.max(s, axis=-1, keepdims=True) * SCALE
            old = m_s[who, h, rows, :]
            new = jnp.maximum(old, jnp.where(kept, top, NEG))
            decay = jnp.exp2(old - new)
            less = jnp.where(kept, new, -NEG)
            p = jnp.exp2(s * SCALE - jnp.concatenate([less] * (T // HD), axis=1))
            m_s[who, h, rows, :] = new
            l_s[who, h, rows, :] = l_s[who, h, rows, :] * decay + jnp.sum(p, axis=-1, keepdims=True)
            acc[who, h, rows, :] = acc[who, h, rows, :] * decay + jnp.dot(
                p.astype(BF16), v, preferred_element_type=F32)

    def own_tile(h, _):
        attend(0, OWN, h, 4)
        return 0

    lax.fori_loop(0, NH, own_tile, 0)

    def arrived(slot, h, part):
        kv_copy(OWN, slot, h, part, kv_s.at[0, h, part], (r, c, mate)).wait_recv()

    def event(at_rank, i):
        first = jnp.where(at_rank < 3, NH, 0)
        crossing = (i >= first) & (i < first + 2 * NH)
        e = jnp.where(crossing, i - first, 0)
        k = lax.rem(e, 2)
        h = jnp.where(crossing, e // 2, i)
        valid = (i >= 0) & (i < first + 2 * NH)
        return valid, crossing, k, jnp.where(valid, h, 0)

    def relay(i, part, other, act):
        valid, crossing, k, h = event(rank, i)
        near = k + 1 >= rank
        slot = jnp.where(crossing, k, 2) + 3 * other
        k_out = jnp.where(crossing, k, 1)

        @pl.when(valid & jnp.where(crossing, rank > 0, rank == 0))
        def _():
            act(kv_copy(slot, k_out + 3 * other, h, part, z_s.at[k_out, other, h, part], onward))

        @pl.when((other == 1) & valid & (near | jnp.logical_not(crossing)))
        def _():
            kind = jnp.where(crossing, k, 2)
            act(kv_copy(slot, MATE + kind, h, part, mate_s.at[kind, h, part], (r, c, mate)))

    def at_copy(slot, h, send, dev):
        return pltpu.make_async_remote_copy(
            src_ref=at.at[slot, h], dst_ref=at.at[slot, h], send_sem=send, recv_sem=at_r.at[slot, h],
            device_id=on_head(dev), device_id_type=MESH)

    def back_copies(h, dev):
        return [
            pltpu.make_async_remote_copy(
                src_ref=buf.at[0, h], dst_ref=buf.at[1, h], send_sem=back_s.at[i, h],
                recv_sem=back_r.at[i, h], device_id=(r, dev, g), device_id_type=MESH)
            for i, buf in enumerate((stats, back))
        ]

    def give_back(h):
        stats[0, h, 0:1, :] = jnp.transpose(m_s[1, h])[0:1, :]
        stats[0, h, 1:2, :] = jnp.transpose(l_s[1, h])[0:1, :]
        back[0, h] = acc[1, h].astype(BF16)
        for copy in back_copies(h, y_to):
            copy.start()

    def finish_head(h):
        @pl.when(has_in)
        def _():
            for copy in back_copies(h, y_from):
                copy.wait_recv()
            m1, l1 = [
                jnp.transpose(jnp.broadcast_to(stats[1, h, i:i + 1, :], (HD, T))) for i in range(2)]
            m0 = m_s[0, h]
            top = jnp.maximum(m0, m1)
            a0, a1 = jnp.exp2(m0 - top), jnp.exp2(m1 - top)
            l_s[0, h] = l_s[0, h] * a0 + l1 * a1
            acc[0, h] = acc[0, h] * a0 + back[1, h].astype(F32) * a1

        at[g, h] = (acc[0, h] / l_s[0, h]).astype(BF16)
        for i, dev in enumerate(peers + [mate]):
            at_copy(g, h, at_s.at[i, h], dev).start()

    def pass_head(h):
        for i, dev in enumerate(peers):
            at_copy(dev, h, at_s.at[i, h], dev).wait_recv()
            at_copy(dev, h, atf_s.at[i, h], mate).start()

    def tick(t, _):
        done = t - LAG - NH - 1

        @pl.when((t == LAG_OWN) & has_out)
        def _():
            mk_copy(y_to).wait_recv()
            for h in range(NH):
                q_copy(h, y_to).wait_recv()

        def turn_of(i, _):
            part, other = i // 2, lax.rem(i, 2)
            valid, crossing, k, h = event(rank, t)

            @pl.when(valid)
            def _():
                arrived(jnp.where(crossing, k, 2) + 3 * other, h, part)
                relay(t, part, other, lambda copy: copy.start())

            ours = lax.rem(i, 2) == 0
            far = i < 2
            at_rank = jnp.where(ours, rank, 3 - rank)
            valid, crossing, k, h = event(at_rank, t - jnp.where(ours, LAG_OWN, LAG))
            near = k + 1 >= at_rank
            downward = jnp.where(ours, core, 1 - core) == 0
            turn = jnp.where(downward, k, 3 - k) - r + 1
            kind = jnp.where(crossing, k, 2)
            slot = jnp.where(ours, kind, MATE + kind)
            side = jnp.where(far, 2 * zh, 2 - 2 * zh)
            offset = jnp.where(crossing, 3 * turn + side, jnp.where(downward, 7, 1))
            needed = valid & jnp.where(crossing, near, True)

            @pl.when(needed & (i == 1))
            def _():
                arrived(slot, h, 0)
                arrived(slot, h, 1)

            @pl.when(needed & jnp.where(far, crossing & has_out, True))
            def _():
                attend(jnp.where(far, 1, 0), slot, h, offset)

            @pl.when((i == 1) & (done >= 0) & (lax.rem(done, 2) == 0) & has_out)
            def _():
                give_back(done // 2)

            return 0

        lax.fori_loop(0, 4, turn_of, 0)

        @pl.when(t < NH - 1)
        def _():
            send_later(t + 1)

        back_in = done - LAG_BACK

        @pl.when((back_in >= 0) & (lax.rem(back_in, 2) == 0))
        def _():
            ready = back_in // 2
            finish_head(ready)

            @pl.when(ready > 0)
            def _():
                pass_head(ready - 1)

        return 0

    lax.fori_loop(0, EVENTS + LAG + LAG_BACK, tick, 0)
    wo_own.wait()
    for i in range(1, NG):
        src = lax.rem(g + i, NG)
        pltpu.make_async_remote_copy(
            src_ref=columns(src), dst_ref=wo.at[src], send_sem=wo_s.at[i], recv_sem=wo_r.at[src],
            device_id=on_head(src), device_id_type=MESH).wait_recv()

    def group(i):
        a = jnp.concatenate([at[i, h] for h in range(NH)], axis=1)
        part = jnp.dot(a, wo[i], preferred_element_type=F32)
        return part.astype(BF16).astype(F32)

    last = NH - 1
    proj[...] = group(g)
    for i, dev in enumerate(peers):
        at_copy(dev, last, at_s.at[i, last], dev).wait_recv()
        at_copy(dev, last, atf_s.at[i, last], mate).start()
        if i < 2:
            proj[...] += group(dev)

    def from_mate(i, _):
        src = mate
        for n, dev in enumerate(peers):
            src = jnp.where(i == n + 1, dev + 1 - 2 * core, src)

        for h in range(NH):
            at_copy(src, h, at_s.at[3, h], mate).wait_recv()
        proj[...] += group(src)
        return 0

    from_mate(0, 0)
    proj[...] += group(peers[2])
    lax.fori_loop(1, 4, from_mate, 0)
    out_ref[...] = (hg[g].astype(F32) + gate_ref[...] * proj[...]).astype(BF16)

    for copy in gathers:
        copy.wait_send()
    for i in range(1, NG):
        wo_copy(i).wait_send()
    for h in range(NH):
        for i, dev in enumerate(peers + [mate]):
            at_copy(g, h, at_s.at[i, h], dev).wait_send()
        for i, dev in enumerate(peers):
            at_copy(dev, h, atf_s.at[i, h], mate).wait_send()

    def sent(i, _):
        for part in range(2):
            for other in range(2):
                relay(i, part, other, lambda copy: copy.wait_send())
        return 0

    lax.fori_loop(0, EVENTS, sent, 0)

    @pl.when(has_in)
    def _():
        mk_copy(y_from).wait_send()
        for h in range(NH):
            q_copy(h, y_from).wait_send()

    @pl.when(has_out)
    def _():
        for h in range(NH):
            for copy in back_copies(h, y_to):
                copy.wait_send()

    for way in range(2):
        for h in range(NH):
            for part in range(2):
                own_copy(way, h, part).wait_send()


def on_device(
    hidden_in, mod_shift, mod_scale, mod_gate, w_qkv, query_gain, key_gain, w_out, window
):
    vmem = pl.BlockSpec(memory_space=pltpu.VMEM)
    hbm = pl.BlockSpec(memory_space=pltpu.HBM)
    dma = pltpu.SemaphoreType.DMA
    out = pl.pallas_call(
        kernel,
        out_shape=jax.ShapeDtypeStruct((T, W), BF16),
        in_specs=[hbm] * 9,
        out_specs=vmem,
        scratch_shapes=[
            pltpu.VMEM((1, W), F32),
            pltpu.VMEM((T, W), F32),
            pltpu.VMEM((1, D), F32),
            pltpu.VMEM((1, D), F32),
            pltpu.VMEM((1, HD), F32),
            pltpu.VMEM((1, HD), F32),
            pltpu.SMEM((1, 1, 9), jnp.int32),
            dma((7,)),
            pltpu.VMEM((NG, T, W), BF16),
            pltpu.VMEM((T, D), BF16),
            pltpu.VMEM((3, D, W), BF16),
            pltpu.VMEM((SLOTS, NH, 2, T, HD), BF16),
            pltpu.VMEM((2, NH, T, HD), BF16),
            pltpu.VMEM((2, NH, T, HD), F32),
            pltpu.VMEM((2, NH, T, HD), F32),
            pltpu.VMEM((2, NH, T, HD), F32),
            pltpu.VMEM((NG, W, W), BF16),
            pltpu.VMEM((NG, NH, T, HD), BF16),
            pltpu.VMEM((2, 16, HD), F32),
            pltpu.VMEM((2, NH, T, HD), BF16),
            pltpu.VMEM((2, NH, 8, T), F32),
            dma((3,)), dma, dma((6,)), dma((2,)), dma((3, 2)), dma((NG, 2)),
            dma((2, NH, 2)), dma((2, 2, NH, 2)), dma((3, NH, 2)), dma((SLOTS, NH, 2)),
            dma((NH,)), dma((NH,)), dma, dma, dma((2, NH)), dma((2, NH)),
            dma((NG,)), dma((NG,)), dma((4, NH)), dma((3, NH)), dma((NG, NH)),
        ],
        compiler_params=pltpu.CompilerParams(
            collective_id=0, has_side_effects=True, vmem_limit_bytes=64 * 1024 * 1024),
        cost_estimate=pl.CostEstimate(
            flops=6_000_000_000, bytes_accessed=10_000_000, transcendentals=4_000_000),
        name="tile_attention",
    )(
        hidden_in.reshape(T, W),
        mod_shift.reshape(1, D),
        mod_scale.reshape(1, D),
        mod_gate,
        jnp.transpose(w_qkv, (1, 0, 2)),
        query_gain.reshape(1, HD),
        key_gain.reshape(1, HD),
        w_out,
        window,
    )
    return out.reshape(hidden_in.shape)


def solution(mesh):
    in_specs = (
        P("row", "col", None, "head"),
        P(),
        P(),
        P("head"),
        P(None, None, "head"),
        P(),
        P(),
        P("head", None),
        P("row", "col", None),
    )
    out_specs = P("row", "col", None, "head")
    return jax.shard_map(
        on_device, mesh=mesh, in_specs=in_specs, out_specs=out_specs, check_vma=False
    )
```

```python
import functools
import math

import jax
import jax.numpy as jnp
from jax import lax
from jax.experimental import pallas as pl
from jax.experimental.pallas import tpu as pltpu
from jax.sharding import PartitionSpec as P

MESH = pl.DeviceIdType.MESH
F32 = jnp.float32
BF16 = jnp.bfloat16
HD = 128
NH = 3
NG = 8
T = 384
W = NH * HD
D = NG * W
ROWS = 4
OWN, MATE = 6, 7
SLOTS = 10
SCALE = math.log2(math.e) / math.sqrt(HD)
NEG = -1e30
EVENTS = 9
LAG_OWN, LAG = 1, 2
LAG_BACK = 1


def kernel(
    x_hbm, shift_hbm, scale_hbm, gate_hbm, w_hbm, qg_hbm, kg_hbm, wo_hbm, win_hbm, out_ref,
    gate_ref, proj,
    shift_ref, scale_ref, qg_ref, kg_ref, win_ref, small_sem, hg, nb, wq, kv, qs, acc, m_s, l_s, wo, at, mk, back, stats,
    w_sem, own_sem, ag_s, agx_s, agf_s, ag_r, kv_s, z_s, mate_s, kv_r, q_s, q_r, mk_s, mk_r, back_s, back_r, wo_s, wo_r, at_s, atf_s, at_r,
):
    r = lax.axis_index("row")
    c = lax.axis_index("col")
    g = lax.axis_index("head")
    y, zh = c // 2, c % 2
    core = g % 2
    mate = g + 1 - 2 * core
    right, left = lax.rem(g + 2, NG), lax.rem(g + 6, NG)
    peers = [lax.rem(g + 2, NG), lax.rem(g + 6, NG), lax.rem(g + 4, NG)]
    x0 = g - core
    z_next = (jnp.where(r < 3, r + 1, 0), jnp.where(r < 3, c, c + 1 - 2 * zh))
    z_prev = (jnp.where(r > 0, r - 1, 3), jnp.where(r > 0, c, c + 1 - 2 * zh))
    rank = jnp.where(core == 0, r, 3 - r)
    onward = (
        jnp.where(core == 0, z_prev[0], z_next[0]), jnp.where(core == 0, z_prev[1], z_next[1]), g)
    y_to = lax.rem(jnp.where(zh == 0, c + 2, c + 6), 8)
    y_from = lax.rem(jnp.where(zh == 0, c + 6, c + 2), 8)
    has_out = jnp.where(zh == 0, y < 3, y > 0)
    has_in = jnp.where(zh == 0, y > 0, y < 3)

    def on_head(i):
        return (r, c, i)

    smalls = [
        pltpu.make_async_copy(src, dst, small_sem.at[i])
        for i, (src, dst) in enumerate([
            (x_hbm, hg.at[g]), (scale_hbm, scale_ref), (shift_hbm, shift_ref),
            (kg_hbm, kg_ref), (qg_hbm, qg_ref), (win_hbm, win_ref), (gate_hbm, gate_ref.at[0])])
    ]
    for copy in smalls:
        copy.start()
    w_copies = [pltpu.make_async_copy(w_hbm.at[j], wq.at[j], w_sem.at[j]) for j in range(3)]
    for j in (1, 2, 0):
        w_copies[j].start()

    def columns(i):
        return wo_hbm.at[:, pl.ds(pl.multiple_of(i * W, W), W)]

    wo_own = pltpu.make_async_copy(columns(g), wo.at[g], own_sem)
    wo_own.start()

    barrier = pltpu.get_barrier_semaphore()
    greeted = [on_head(lax.rem(g + i, NG)) for i in range(1, NG)]
    greeted += [z + (x0 + k,) for z in (z_prev, z_next) for k in range(2)]
    greeted += [(r, y_to, g), (r, y_from, g)]
    for dev in greeted:
        pl.semaphore_signal(barrier, inc=1, device_id=dev, device_id_type=MESH)
    pl.semaphore_wait(barrier, len(greeted))

    half = T // 2

    def ag_copy(slot, part, send, dev):
        piece = hg.at[slot, pl.ds(part * half, half), :]
        return pltpu.make_async_remote_copy(
            src_ref=piece, dst_ref=piece, send_sem=send, recv_sem=ag_r.at[slot, part],
            device_id=on_head(dev), device_id_type=MESH)

    gathers = []

    def gather(slot, part, send, dev):
        copy = ag_copy(slot, part, send, dev)
        copy.start()
        gathers.append(copy)

    def gathered(slot, part):
        ag_copy(slot, part, ag_s.at[0], mate).wait_recv()

    smalls[0].wait()
    for i in range(2):
        gather(g, i, ag_s.at[i], right)
        gather(g, 1 - i, ag_s.at[2 + i], left)
    for part in range(2):
        gather(g, part, ag_s.at[4 + part], mate)
    m_s[...] = jnp.full_like(m_s, NEG)
    l_s[...] = jnp.zeros_like(l_s)
    acc[...] = jnp.zeros_like(acc)
    gathered(left, 0)
    gather(left, 0, agx_s.at[0], right)
    gathered(right, 1)
    gather(right, 1, agx_s.at[1], left)
    gather(left, 0, agf_s.at[0, 0], mate)
    gather(right, 1, agf_s.at[1, 1], mate)
    gathered(left, 1)
    gather(left, 1, agf_s.at[0, 1], mate)
    gathered(right, 0)
    gather(right, 0, agf_s.at[1, 0], mate)
    for part in range(2):
        gathered(peers[2], part)
        gather(peers[2], part, agf_s.at[2, part], mate)
    for dev in [mate] + [dev + 1 - 2 * core for dev in peers]:
        for part in range(2):
            gathered(dev, part)
    for copy in smalls[1:]:
        copy.wait()

    step = 32

    def norm_rows(i, _):
        rows = pl.ds(pl.multiple_of(i * step, step), step)
        parts = [hg[j, rows, :].astype(F32) for j in range(NG)]
        total = parts[0]
        for part in parts[1:]:
            total = total + part
        center = jnp.sum(total, axis=-1, keepdims=True) * (1.0 / D)
        squares = None
        for part in parts:
            off = part - center
            squares = off * off if squares is None else squares + off * off
        spread = jnp.sum(squares, axis=-1, keepdims=True) * (1.0 / D)
        inv = lax.rsqrt(spread + 1e-6)
        for j in range(NG):
            cols = slice(j * W, (j + 1) * W)
            nb[rows, cols] = (
                (parts[j] - center) * inv * (1.0 + scale_ref[:, cols]) + shift_ref[:, cols]
            ).astype(BF16)
        return 0

    lax.fori_loop(0, T // step, norm_rows, 0, unroll=2)

    def kv_copy(src, dst, h, part, send, dev):
        return pltpu.make_async_remote_copy(
            src_ref=kv.at[src, h, part], dst_ref=kv.at[dst, h, part],
            send_sem=send, recv_sem=kv_r.at[dst, h, part],
            device_id=dev, device_id_type=MESH)

    def own_copy(way, h, part):
        first = jnp.where(r == 0, 0, 2) if way == 0 else jnp.where(r == 3, 0, 2)
        slot = first + 3 * jnp.where(core == way, 0, 1)
        to = z_prev if way == 0 else z_next
        return kv_copy(OWN, slot, h, part, kv_s.at[way, h, part], to + (x0 + way,))

    ranks = (r, 3 - r)

    def send_own(h, part):
        for way in range(2):
            @pl.when((h == 0) | (ranks[way] > 0))
            def _():
                own_copy(way, h, part).start()

    def send_later(h):
        for way in range(2):
            @pl.when(ranks[way] == 0)
            def _():
                for part in range(2):
                    own_copy(way, h, part).start()

    def project(j):
        w_copies[j].wait()
        return jnp.dot(nb[...], wq[j], preferred_element_type=F32)

    def head_norm(values, gain):
        mean = jnp.mean(values * values, axis=-1, keepdims=True)
        return (values * lax.rsqrt(mean + 1e-6) * gain).astype(BF16)

    keys = project(1)
    for h in range(NH):
        kv[OWN, h, 0] = head_norm(keys[:, h * HD:(h + 1) * HD], kg_ref[...])
        send_own(h, 0)
    values = project(2)
    for h in range(NH):
        kv[OWN, h, 1] = values[:, h * HD:(h + 1) * HD].astype(BF16)
        send_own(h, 1)

    def q_copy(h, dev):
        return pltpu.make_async_remote_copy(
            src_ref=qs.at[0, h], dst_ref=qs.at[1, h], send_sem=q_s.at[h], recv_sem=q_r.at[h],
            device_id=(r, dev, g), device_id_type=MESH)

    def mk_copy(dev):
        return pltpu.make_async_remote_copy(
            src_ref=mk.at[0], dst_ref=mk.at[1], send_sem=mk_s, recv_sem=mk_r,
            device_id=(r, dev, g), device_id_type=MESH)

    for i in range(9):
        mk[0, i:i + 1, :] = jnp.full((1, HD), win_ref[0, 0, i].astype(F32))

    @pl.when(has_in)
    def _():
        mk_copy(y_from).start()

    queries = project(0)
    for h in range(NH):
        qs[0, h] = head_norm(queries[:, h * HD:(h + 1) * HD], qg_ref[...])

        @pl.when(has_in)
        def _():
            q_copy(h, y_from).start()

    def wo_copy(i):
        dev = lax.rem(g + i, NG)
        return pltpu.make_async_remote_copy(
            src_ref=columns(dev), dst_ref=wo.at[g], send_sem=wo_s.at[i], recv_sem=wo_r.at[g],
            device_id=on_head(dev), device_id_type=MESH)

    for i in range(1, NG):
        wo_copy(i).start()

    block = 384

    def attend(who, slot, h, offset):
        kept = mk[who, pl.ds(offset, 1), :] > 0
        k = kv[slot, h, 0]
        v = kv[slot, h, 1]
        for i in range(T // block):
            rows = slice(i * block, (i + 1) * block)
            s = lax.dot_general(
                qs[who, h, rows, :], k, (((1,), (1,)), ((), ())), preferred_element_type=F32)
            top = jnp.max(s, axis=-1, keepdims=True) * SCALE
            old = m_s[who, h, rows, :]
            new = jnp.maximum(old, jnp.where(kept, top, NEG))
            decay = jnp.exp2(old - new)
            less = jnp.where(kept, new, -NEG)
            p = jnp.exp2(s * SCALE - jnp.concatenate([less] * (T // HD), axis=1))
            m_s[who, h, rows, :] = new
            l_s[who, h, rows, :] = l_s[who, h, rows, :] * decay + jnp.sum(p, axis=-1, keepdims=True)
            acc[who, h, rows, :] = acc[who, h, rows, :] * decay + jnp.dot(
                p.astype(BF16), v, preferred_element_type=F32)

    def own_tile(h, _):
        attend(0, OWN, h, 4)
        return 0

    lax.fori_loop(0, NH, own_tile, 0)

    def arrived(slot, h, part):
        kv_copy(OWN, slot, h, part, kv_s.at[0, h, part], (r, c, mate)).wait_recv()

    def event(at_rank, i):
        first = jnp.where(at_rank < 3, NH, 0)
        crossing = (i >= first) & (i < first + 2 * NH)
        e = jnp.where(crossing, i - first, 0)
        k = lax.rem(e, 2)
        h = jnp.where(crossing, e // 2, i)
        valid = (i >= 0) & (i < first + 2 * NH)
        return valid, crossing, k, jnp.where(valid, h, 0)

    def relay(i, part, other, act):
        valid, crossing, k, h = event(rank, i)
        near = k + 1 >= rank
        slot = jnp.where(crossing, k, 2) + 3 * other
        k_out = jnp.where(crossing, k, 1)

        @pl.when(valid & jnp.where(crossing, rank > 0, rank == 0))
        def _():
            act(kv_copy(slot, k_out + 3 * other, h, part, z_s.at[k_out, other, h, part], onward))

        @pl.when((other == 1) & valid & (near | jnp.logical_not(crossing)))
        def _():
            kind = jnp.where(crossing, k, 2)
            act(kv_copy(slot, MATE + kind, h, part, mate_s.at[kind, h, part], (r, c, mate)))

    def at_copy(slot, h, send, dev):
        return pltpu.make_async_remote_copy(
            src_ref=at.at[slot, h], dst_ref=at.at[slot, h], send_sem=send, recv_sem=at_r.at[slot, h],
            device_id=on_head(dev), device_id_type=MESH)

    def back_copies(h, dev):
        return [
            pltpu.make_async_remote_copy(
                src_ref=buf.at[0, h], dst_ref=buf.at[1, h], send_sem=back_s.at[i, h],
                recv_sem=back_r.at[i, h], device_id=(r, dev, g), device_id_type=MESH)
            for i, buf in enumerate((stats, back))
        ]

    def give_back(h):
        stats[0, h, 0:1, :] = jnp.transpose(m_s[1, h])[0:1, :]
        stats[0, h, 1:2, :] = jnp.transpose(l_s[1, h])[0:1, :]
        back[0, h] = acc[1, h].astype(BF16)
        for copy in back_copies(h, y_to):
            copy.start()

    def finish_head(h):
        @pl.when(has_in)
        def _():
            for copy in back_copies(h, y_from):
                copy.wait_recv()
            m1, l1 = [
                jnp.transpose(jnp.broadcast_to(stats[1, h, i:i + 1, :], (HD, T))) for i in range(2)]
            m0 = m_s[0, h]
            top = jnp.maximum(m0, m1)
            a0, a1 = jnp.exp2(m0 - top), jnp.exp2(m1 - top)
            l_s[0, h] = l_s[0, h] * a0 + l1 * a1
            acc[0, h] = acc[0, h] * a0 + back[1, h].astype(F32) * a1

        at[g, h] = (acc[0, h] / l_s[0, h]).astype(BF16)
        for i, dev in enumerate(peers + [mate]):
            at_copy(g, h, at_s.at[i, h], dev).start()

    def pass_head(h):
        for i, dev in enumerate(peers):
            at_copy(dev, h, at_s.at[i, h], dev).wait_recv()
            at_copy(dev, h, atf_s.at[i, h], mate).start()

    def tick(t, _):
        done = t - LAG - NH - 1

        @pl.when((t == LAG_OWN) & has_out)
        def _():
            mk_copy(y_to).wait_recv()
            for h in range(NH):
                q_copy(h, y_to).wait_recv()

        def turn_of(i, _):
            part, other = i // 2, lax.rem(i, 2)
            valid, crossing, k, h = event(rank, t)

            @pl.when(valid)
            def _():
                arrived(jnp.where(crossing, k, 2) + 3 * other, h, part)
                relay(t, part, other, lambda copy: copy.start())

            ours = lax.rem(i, 2) == 0
            far = i < 2
            at_rank = jnp.where(ours, rank, 3 - rank)
            valid, crossing, k, h = event(at_rank, t - jnp.where(ours, LAG_OWN, LAG))
            near = k + 1 >= at_rank
            downward = jnp.where(ours, core, 1 - core) == 0
            turn = jnp.where(downward, k, 3 - k) - r + 1
            kind = jnp.where(crossing, k, 2)
            slot = jnp.where(ours, kind, MATE + kind)
            side = jnp.where(far, 2 * zh, 2 - 2 * zh)
            offset = jnp.where(crossing, 3 * turn + side, jnp.where(downward, 7, 1))
            needed = valid & jnp.where(crossing, near, True)

            @pl.when(needed & (i == 1))
            def _():
                arrived(slot, h, 0)
                arrived(slot, h, 1)

            @pl.when(needed & jnp.where(far, crossing & has_out, True))
            def _():
                attend(jnp.where(far, 1, 0), slot, h, offset)

            @pl.when((i == 1) & (done >= 0) & (lax.rem(done, 2) == 0) & has_out)
            def _():
                give_back(done // 2)

            return 0

        lax.fori_loop(0, 4, turn_of, 0)

        @pl.when(t < NH - 1)
        def _():
            send_later(t + 1)

        back_in = done - LAG_BACK

        @pl.when((back_in >= 0) & (lax.rem(back_in, 2) == 0))
        def _():
            ready = back_in // 2
            finish_head(ready)

            @pl.when(ready > 0)
            def _():
                pass_head(ready - 1)

        return 0

    lax.fori_loop(0, EVENTS + LAG + LAG_BACK, tick, 0)
    wo_own.wait()
    for i in range(1, NG):
        src = lax.rem(g + i, NG)
        pltpu.make_async_remote_copy(
            src_ref=columns(src), dst_ref=wo.at[src], send_sem=wo_s.at[i], recv_sem=wo_r.at[src],
            device_id=on_head(src), device_id_type=MESH).wait_recv()

    def group(i):
        a = jnp.concatenate([at[i, h] for h in range(NH)], axis=1)
        part = jnp.dot(a, wo[i], preferred_element_type=F32)
        return part.astype(BF16).astype(F32)

    last = NH - 1
    proj[...] = group(g)
    for i, dev in enumerate(peers):
        at_copy(dev, last, at_s.at[i, last], dev).wait_recv()
        at_copy(dev, last, atf_s.at[i, last], mate).start()
        if i < 2:
            proj[...] += group(dev)

    def from_mate(i, _):
        src = mate
        for n, dev in enumerate(peers):
            src = jnp.where(i == n + 1, dev + 1 - 2 * core, src)

        for h in range(NH):
            at_copy(src, h, at_s.at[3, h], mate).wait_recv()
        proj[...] += group(src)
        return 0

    from_mate(0, 0)
    proj[...] += group(peers[2])
    lax.fori_loop(1, 4, from_mate, 0)
    out_ref[...] = (hg[g].astype(F32) + gate_ref[...] * proj[...]).astype(BF16)

    for copy in gathers:
        copy.wait_send()
    for i in range(1, NG):
        wo_copy(i).wait_send()
    for h in range(NH):
        for i, dev in enumerate(peers + [mate]):
            at_copy(g, h, at_s.at[i, h], dev).wait_send()
        for i, dev in enumerate(peers):
            at_copy(dev, h, atf_s.at[i, h], mate).wait_send()

    def sent(i, _):
        for part in range(2):
            for other in range(2):
                relay(i, part, other, lambda copy: copy.wait_send())
        return 0

    lax.fori_loop(0, EVENTS, sent, 0)

    @pl.when(has_in)
    def _():
        mk_copy(y_from).wait_send()
        for h in range(NH):
            q_copy(h, y_from).wait_send()

    @pl.when(has_out)
    def _():
        for h in range(NH):
            for copy in back_copies(h, y_to):
                copy.wait_send()

    for way in range(2):
        for h in range(NH):
            for part in range(2):
                own_copy(way, h, part).wait_send()


def on_device(
    hidden_in, mod_shift, mod_scale, mod_gate, w_qkv, query_gain, key_gain, w_out, window
):
    vmem = pl.BlockSpec(memory_space=pltpu.VMEM)
    hbm = pl.BlockSpec(memory_space=pltpu.HBM)
    dma = pltpu.SemaphoreType.DMA
    out = pl.pallas_call(
        kernel,
        out_shape=jax.ShapeDtypeStruct((T, W), BF16),
        in_specs=[hbm] * 9,
        out_specs=vmem,
        scratch_shapes=[
            pltpu.VMEM((1, W), F32),
            pltpu.VMEM((T, W), F32),
            pltpu.VMEM((1, D), F32),
            pltpu.VMEM((1, D), F32),
            pltpu.VMEM((1, HD), F32),
            pltpu.VMEM((1, HD), F32),
            pltpu.SMEM((1, 1, 9), jnp.int32),
            dma((7,)),
            pltpu.VMEM((NG, T, W), BF16),
            pltpu.VMEM((T, D), BF16),
            pltpu.VMEM((3, D, W), BF16),
            pltpu.VMEM((SLOTS, NH, 2, T, HD), BF16),
            pltpu.VMEM((2, NH, T, HD), BF16),
            pltpu.VMEM((2, NH, T, HD), F32),
            pltpu.VMEM((2, NH, T, HD), F32),
            pltpu.VMEM((2, NH, T, HD), F32),
            pltpu.VMEM((NG, W, W), BF16),
            pltpu.VMEM((NG, NH, T, HD), BF16),
            pltpu.VMEM((2, 16, HD), F32),
            pltpu.VMEM((2, NH, T, HD), BF16),
            pltpu.VMEM((2, NH, 8, T), F32),
            dma((3,)), dma, dma((6,)), dma((2,)), dma((3, 2)), dma((NG, 2)),
            dma((2, NH, 2)), dma((2, 2, NH, 2)), dma((3, NH, 2)), dma((SLOTS, NH, 2)),
            dma((NH,)), dma((NH,)), dma, dma, dma((2, NH)), dma((2, NH)),
            dma((NG,)), dma((NG,)), dma((4, NH)), dma((3, NH)), dma((NG, NH)),
        ],
        compiler_params=pltpu.CompilerParams(
            collective_id=0, has_side_effects=True, vmem_limit_bytes=64 * 1024 * 1024),
        cost_estimate=pl.CostEstimate(
            flops=6_000_000_000, bytes_accessed=10_000_000, transcendentals=4_000_000),
        name="tile_attention",
    )(
        hidden_in.reshape(T, W),
        mod_shift.reshape(1, D),
        mod_scale.reshape(1, D),
        mod_gate,
        jnp.transpose(w_qkv, (1, 0, 2)),
        query_gain.reshape(1, HD),
        key_gain.reshape(1, HD),
        w_out,
        window,
    )
    return out.reshape(hidden_in.shape)


def solution(mesh):
    in_specs = (
        P("row", "col", None, "head"),
        P(),
        P(),
        P("head"),
        P(None, None, "head"),
        P(),
        P(),
        P("head", None),
        P("row", "col", None),
    )
    out_specs = P("row", "col", None, "head")
    return jax.shard_map(
        on_device, mesh=mesh, in_specs=in_specs, out_specs=out_specs, check_vma=False
    )
```
